256 devices in a mesh: rep: 32 (over y, z_hi, x), tp: 8 (over z_lo, core).
Axes of the slice: x: 4, y: 4, z: 8 (z_hi: 2, z_lo: 4; z = z_hi * 4 + z_lo), core: 2. Of those that a mesh axis runs over, the one named last changes fastest.
Arguments:
- queries: bfloat16 [1024, 4096], P('rep', 'tp'), may hold values from -150 to 150
- k_cache: bfloat16 [1024, 128, 1024], P('rep', None, 'tp'), may hold values from -6.5 to 6.5
- v_cache: bfloat16 [1024, 128, 1024], P('rep', None, 'tp'), may hold values from -24 to 24
- new_keys: bfloat16 [1024, 1024], P('rep', 'tp'), may hold values from -6 to 6
- new_values: bfloat16 [1024, 1024], P('rep', 'tp'), may hold values from -24 to 24
- kv_len: int32 [1024], P('rep'), may hold values from 2 to 127
- send_rows: int32 [32, 8], P('rep'), may hold values from -1 to 31, as said below
- recv_rows: int32 [32, 8], P('rep'), may hold values from -1 to 31, as said below
- out_weight: bfloat16 [8192, 4096], P(None, 'tp'), may hold values from -0.09375 to 0.09375
- adapter_down: bfloat16 [256, 64, 4096], P('rep', None, 'tp'), may hold values from -0.09375 to 0.09375
- adapter_up: bfloat16 [256, 64, 8192], P('rep', None, 'tp'), may hold values from -0.75 to 0.75
- sectioned_down: bfloat16 [32, 64, 4096], P('rep', None, 'tp'), may hold values from -0.09375 to 0.09375
- sectioned_up: bfloat16 [32, 64, 8192], P('rep', None, 'tp'), may hold values from -0.75 to 0.75
- install: int32 [32, 8], P('rep'), may hold values from -1 to 31
- adapter_slot: int32 [1024], P('rep'), may hold values from 0 to 7
Outputs:
- mixed: bfloat16 [1024, 8192], P('rep', 'tp')
The draws below stay inside these ranges and needn't reach their ends.
Inputs may be any that keep to these rules, and one draw needn't show every extreme that they name: `send_rows`: column j of a replica's row names a request that moves to the replica that many places after it (wrapping): 1 place for j // 2 = 0, else (j // 2 + 1) * 4 places; the named requests of one row are distinct; at most 2 requests go from one replica to another, and some replica receives exactly 2 from each of the 4 replicas that send to it. recv_rows[d, j] >= 0 exactly where the column j entry of the replica that column's distance before d in send_rows is >= 0; the named rows of one replica are distinct.
All inputs are finite; a program needn't handle non-finite values.
Results may differ from the reference program's by a relative error of at most 0.02.
Values may be sent and summed in bfloat16 or wider, within the bound.
A program may use at most 64 MiB of HBM per device.

```python
import jax
import jax.numpy as jnp
from jax import lax

MODEL_WIDTH = 8192
KVH = 8
HD = 128
QH = 32
ADAPTER_RANK = 64
RESIDENT_SLOTS = 8
SECTION = 1
LMAX = 128
SPAN = 4
CAP = 2
MIG = 6
REQ = 32
QW = 4096
REQ_ALL = 1024
HOP = 4
N_REP = 32


def cache_keys(key):
    return jnp.clip(jax.random.normal(key, (REQ_ALL, LMAX, KVH * HD), jnp.float32), -6.0, 6.0)


def draw_k_cache(key, part):
    base_output = cache_keys(key)
    return base_output.astype(jnp.bfloat16)


def draw_queries(key, part):
    key = jax.random.fold_in(key, 12)
    drawn = jnp.clip(jax.random.normal(key, (REQ_ALL, QH * HD), jnp.float32), -6.0, 6.0)
    return drawn.astype(jnp.bfloat16)


def draw_kv_len(key, part):
    key = jax.random.fold_in(key, 13)
    values = jax.random.randint(key, (REQ_ALL,), 2, LMAX)
    return values.at[0].set(LMAX - 1).astype(jnp.int32)


def column_distance(column, hop):
    group = column // CAP
    return jnp.where(group == 0, 1, (group + 1) * hop)


def migration_plan(key):
    replicas = REQ_ALL // REQ
    hop = replicas // (2 * SPAN)
    width = SPAN * CAP
    key_off, key_req, key_slot = jax.random.split(key, 3)
    groups = jax.random.randint(key_off, (replicas, MIG), 1, SPAN + 1)
    row = jnp.arange(replicas)
    forced_dist = (1 - row) % replicas
    far = forced_dist // hop
    far_ok = (forced_dist % hop == 0) & (far >= 2) & (far <= SPAN)
    forced = jnp.where(forced_dist == 1, 1, jnp.where(far_ok, far, 0))
    valid = forced >= 1
    pinned = valid[:, None] & (jnp.arange(MIG) < CAP)[None, :]
    groups = jnp.where(pinned, forced[:, None], groups)
    onehot = (groups[:, :, None] == jnp.arange(1, SPAN + 1)[None, None, :]).astype(jnp.int32)
    earlier = jnp.cumsum(onehot, axis=1) - onehot
    rank = jnp.sum(earlier * onehot, axis=2)
    keep = rank < CAP
    scores = jax.random.randint(key_req, (replicas, REQ), 0, 1 << 20) * REQ + jnp.arange(REQ)[None, :]
    leaving = jnp.argsort(scores, axis=1)[:, :MIG]
    place = (groups - 1) * CAP + rank
    hit = ((place[:, :, None] == jnp.arange(width)[None, None, :]) & keep[:, :, None]).astype(jnp.int32)
    send = jnp.where(jnp.sum(hit, axis=1) > 0, jnp.sum(hit * (leaving[:, :, None] + 1), axis=1) - 1, -1)
    column = jnp.arange(width)
    source = (row[:, None] - column_distance(column, hop)[None, :]) % replicas
    active = send[source, jnp.broadcast_to(column[None, :], source.shape)] >= 0
    slot_scores = jax.random.randint(key_slot, (replicas, REQ), 0, 1 << 20) * REQ + jnp.arange(REQ)[None, :]
    arriving = jnp.argsort(slot_scores, axis=1)[:, :width]
    recv = jnp.where(active, arriving, -1)
    return (send.astype(jnp.int32), recv.astype(jnp.int32))


def draw_send_rows(key, part):
    plan = migration_plan(key)
    return plan[0]


def draw_recv_rows(key, part):
    plan = migration_plan(key)
    return plan[1]


def draw_install(key, part):
    key = jax.random.fold_in(key, 16)
    replicas = REQ_ALL // REQ
    sectioned = replicas * SECTION
    raw = jax.random.randint(key, (replicas, RESIDENT_SLOTS), 0, 2 * sectioned) - sectioned
    picks = jnp.where(raw < 0, -1, raw)
    picks = picks.at[0, 0].set(sectioned - 1)
    picks = picks.at[0, 1].set(-1)
    return picks.astype(jnp.int32)


def set_ends(drawn, rng, least, high):
    dims = drawn.shape
    spot = [jax.random.randint(jax.random.fold_in(rng, axis), (), 0, dims[axis]) for axis in range(len(dims))]
    drawn = drawn.at[tuple(spot)].set(least)
    longest = dims.index(max(dims))
    spot[longest] = (spot[longest] + 1) % dims[longest]
    return drawn.at[tuple(spot)].set(high)


def shard_levels(key, dims, cuts, least, largest):
    level = 1.0
    for axis_at, parts in cuts:
        steps = jax.random.uniform(jax.random.fold_in(jax.random.fold_in(key, 6), axis_at), (parts,), jnp.float32, least / len(cuts), largest / len(cuts))
        level = level * jnp.repeat(jnp.exp(steps), dims[axis_at] // parts).reshape((-1,) + (1,) * (len(dims) - 1 - axis_at))
    return level


def gaussian(key, extent, scale, limit, pieces=(), kind=jnp.bfloat16):
    result = jax.random.normal(key, extent, jnp.float32) * scale
    if len(pieces) > 0:
        result = shard_levels(key, extent, pieces, -0.22, 0.18) * result
    return jnp.clip(result, min=-limit, max=limit).astype(kind)


def setup_inputs(seed: int = 0) -> dict:
    splits = jax.random.split(jax.random.key(seed), 16)
    queries = draw_queries(jax.random.fold_in(splits[15], 71), 0)
    k_cache = draw_k_cache(jax.random.fold_in(splits[15], 71), 0)
    v_cache = gaussian(splits[2], (REQ_ALL, LMAX, KVH * HD), 4.0, 24.0, ((0, 32), (2, 8)))
    new_keys = gaussian(splits[3], (REQ_ALL, KVH * HD), 1.0, 6.0, ((0, 32), (1, 8)))
    new_values = gaussian(splits[4], (REQ_ALL, KVH * HD), 4.0, 24.0, ((0, 32), (1, 8)))
    kv_len = draw_kv_len(jax.random.fold_in(splits[15], 71), 0)
    send_rows = draw_send_rows(jax.random.fold_in(splits[15], 71), 0)
    recv_rows = draw_recv_rows(jax.random.fold_in(splits[15], 71), 0)
    out_weight = gaussian(splits[8], (MODEL_WIDTH, QW), QW ** -0.5, 0.09375, ((1, 8),))
    adapter_down = gaussian(splits[9], (N_REP * RESIDENT_SLOTS, ADAPTER_RANK, QW), QW ** -0.5, 0.09375, ((0, 32), (2, 8)))
    adapter_up = gaussian(splits[10], (N_REP * RESIDENT_SLOTS, ADAPTER_RANK, MODEL_WIDTH), ADAPTER_RANK ** -0.5, 0.75, ((0, 32), (2, 8)))
    sectioned_down = gaussian(splits[11], (N_REP * SECTION, ADAPTER_RANK, QW), QW ** -0.5, 0.09375, ((0, 32), (2, 8)))
    sectioned_up = gaussian(splits[12], (N_REP * SECTION, ADAPTER_RANK, MODEL_WIDTH), ADAPTER_RANK ** -0.5, 0.75, ((0, 32), (2, 8)))
    install = draw_install(jax.random.fold_in(splits[15], 71), 0)
    adapter_slot = set_ends(jax.random.randint(splits[14], (REQ_ALL,), 0, RESIDENT_SLOTS), jax.random.fold_in(splits[14], 1), 0, RESIDENT_SLOTS - 1).astype(jnp.int32)
    return {"queries": queries, "k_cache": k_cache, "v_cache": v_cache, "new_keys": new_keys, "new_values": new_values, "kv_len": kv_len, "send_rows": send_rows, "recv_rows": recv_rows, "out_weight": out_weight, "adapter_down": adapter_down, "adapter_up": adapter_up, "sectioned_down": sectioned_down, "sectioned_up": sectioned_up, "install": install, "adapter_slot": adapter_slot}


def migrate_index(send_rows, recv_rows):
    width = send_rows.shape[1]
    column = jnp.arange(width, dtype=jnp.int32)
    group = column // CAP
    offset = jnp.where(group == 0, 1, (group + 1) * HOP).astype(jnp.int32)
    dest = jnp.arange(N_REP, dtype=jnp.int32)[:, None]
    source = (dest - offset[None, :]) % N_REP
    moved = send_rows[source, jnp.broadcast_to(column[None, :], source.shape)]
    root = (source * REQ + jnp.maximum(moved, 0)).astype(jnp.int32)
    target = jnp.where(recv_rows >= 0, dest * REQ + recv_rows, N_REP * REQ).astype(jnp.int32)
    start = jnp.arange(N_REP * REQ, dtype=jnp.int32)
    return start.at[target.reshape(-1)].set(root.reshape(-1), mode="drop")


def install_rows(resident, sectioned, install):
    picks = install.reshape(-1)
    chosen = sectioned[jnp.maximum(picks, 0)]
    return jnp.where((picks >= 0)[:, None, None], chosen, resident)


def attend(queries, keys, values, new_key, new_value, lengths):
    groups = QH // KVH
    query = queries.astype(jnp.float32).reshape(REQ, KVH, groups, HD)
    key_rows = keys.astype(jnp.float32).reshape(REQ, LMAX, KVH, HD)
    value_rows = values.astype(jnp.float32).reshape(REQ, LMAX, KVH, HD)
    own_key = new_key.astype(jnp.float32).reshape(REQ, KVH, HD)
    own_value = new_value.astype(jnp.float32).reshape(REQ, KVH, HD)
    scale = HD ** -0.5
    scores = jnp.einsum("rkgd,rlkd->rkgl", query, key_rows) * scale
    live = jnp.arange(LMAX)[None, :] < lengths[:, None]
    scores = jnp.where(live[:, None, None, :], scores, -jnp.inf)
    own = jnp.einsum("rkgd,rkd->rkg", query, own_key) * scale
    top = jnp.maximum(jnp.max(scores, axis=-1), own)
    weights = jnp.exp(scores - top[..., None])
    own_weight = jnp.exp(own - top)
    total = jnp.sum(weights, axis=-1) + own_weight
    weights_b = lax.optimization_barrier(weights.astype(jnp.bfloat16)).astype(jnp.float32)
    own_b = lax.optimization_barrier(own_weight.astype(jnp.bfloat16)).astype(jnp.float32)
    summed = jnp.einsum("rkgl,rlkd->rkgd", weights_b, value_rows) + own_b[..., None] * own_value[:, :, None, :]
    return (summed / total[..., None]).astype(jnp.bfloat16).reshape(REQ, QH * HD)


def reference(queries, k_cache, v_cache, new_keys, new_values, kv_len, send_rows, recv_rows, out_weight, adapter_down, adapter_up, sectioned_down, sectioned_up, install, adapter_slot):
    source = migrate_index(send_rows, recv_rows)
    keys = k_cache[source]
    values = v_cache[source]
    lengths = kv_len[source]
    down = install_rows(adapter_down, sectioned_down, install)
    up = install_rows(adapter_up, sectioned_up, install)

    def replica(items):
        query, key_rows, value_rows, own_key, own_value, length, down_maps, up_projection_weights, slot = items
        attn = attend(query, key_rows, value_rows, own_key, own_value, length)
        partial_value = jnp.einsum("rq,skq->rsk", attn.astype(jnp.float32), down_maps.astype(jnp.float32))
        onehot = (slot[:, None] == jnp.arange(RESIDENT_SLOTS)[None, :]).astype(jnp.float32)
        down_projected = (partial_value * onehot[:, :, None]).reshape(REQ, RESIDENT_SLOTS * ADAPTER_RANK).astype(jnp.bfloat16)
        low_rank_delta = jnp.dot(down_projected, up_projection_weights.reshape(RESIDENT_SLOTS * ADAPTER_RANK, MODEL_WIDTH), preferred_element_type=jnp.float32)
        base_output = lax.dot_general(attn, out_weight, (((1,), (1,)), ((), ())), preferred_element_type=jnp.float32)
        return (base_output + low_rank_delta).astype(jnp.bfloat16)

    items = (queries.reshape(N_REP, REQ, QW), keys.reshape(N_REP, REQ, LMAX, KVH * HD),
             values.reshape(N_REP, REQ, LMAX, KVH * HD), new_keys.reshape(N_REP, REQ, KVH * HD),
             new_values.reshape(N_REP, REQ, KVH * HD), lengths.reshape(N_REP, REQ),
             down.reshape(N_REP, RESIDENT_SLOTS, ADAPTER_RANK, QW), up.reshape(N_REP, RESIDENT_SLOTS, ADAPTER_RANK, MODEL_WIDTH),
             adapter_slot.reshape(N_REP, REQ))
    mixed = lax.map(replica, items)
    return mixed.reshape(REQ_ALL, MODEL_WIDTH)
```

```python
import functools

import jax
import jax.numpy as jnp
from jax import lax
from jax.experimental import pallas as pl
from jax.experimental.pallas import tpu as pltpu
from jax.sharding import PartitionSpec as P

MESH = pl.DeviceIdType.MESH
F32 = jnp.float32
BF16 = jnp.bfloat16

HD = 128
HEADS = 4
REQ = 32
LMAX = 128
RANK = 64
SLOTS = 8
SPAN = 4
CAP = 2
REP = 32
TP = 8
ROW = 4
QW = HEADS * HD
OUT = 1024
RANK_PART = RANK // ROW
OUT_PART = OUT // ROW
SCALE = HD**-0.5
DISTANCES = (1, 8, 12, 16)


def iota(shape, dim):
    return lax.broadcasted_iota(jnp.int32, shape, dim)


def dot(a, b):
    return lax.dot_general(a, b, (((1,), (0,)), ((), ())), preferred_element_type=F32)


def dot_nt(a, b):
    return lax.dot_general(a, b, (((1,), (1,)), ((), ())), preferred_element_type=F32)


def remote(src, dst, ssem, rsem, device):
    return pltpu.make_async_remote_copy(
        src_ref=src,
        dst_ref=dst,
        send_sem=ssem,
        recv_sem=rsem,
        device_id=device,
        device_id_type=MESH,
    )


def softmax_parts(scores, own, live):
    scores = jnp.where(live, scores * SCALE, -jnp.inf)
    own = own * SCALE
    top = jnp.maximum(jnp.max(scores, axis=1, keepdims=True), own)
    weights = jnp.exp(scores - top)
    own_weight = jnp.exp(own - top)
    total = jnp.sum(weights, axis=1, keepdims=True) + own_weight
    return weights.astype(BF16), own_weight.astype(BF16).astype(F32), total


def to_column(row, rows):
    spread = jnp.where(iota((rows, 128), 0) == iota((rows, 128), 1), row, 0)
    return jnp.sum(spread.astype(F32), axis=1, keepdims=True).astype(jnp.int32)


def kernel(
    q_ref,
    k_hbm,
    v_hbm,
    nk_ref,
    nv_ref,
    len_row,
    slot_row,
    len_s,
    send_s,
    recv_s,
    install_s,
    w_hbm,
    adown_hbm,
    aup_hbm,
    sdown_hbm,
    sup_hbm,
    out_ref,
    kbuf,
    vbuf,
    wbuf,
    adown,
    aup,
    sdn,
    sup,
    qout,
    qin,
    meta,
    res,
    mig,
    loc,
    merged,
    obuf,
    fold,
    perm,
    msg,
    msg_sib,
    bc,
    sexp,
    dlt_out,
    dlt_in,
    sib_out,
    sib_in,
    rs_own,
    rs_out,
    rs_in,
    load_sem,
    s1_local,
    s1_ssem,
    s1_rsem,
    s2_ssem,
    s2_rsem,
    q_ssem,
    q_rsem,
    meta_ssem,
    meta_rsem,
    mig_ssem,
    mig_rsem,
    loc_ssem,
    loc_rsem,
    msg_sem,
    bc_ssem,
    bc_rsem,
    dlt_ssem,
    dlt_rsem,
    sib_ssem,
    sib_rsem,
    rs_ssem,
    rs_rsem,
):
    r = lax.axis_index("rep")
    t = lax.axis_index("tp")
    x = r % 4
    zh = (r // 4) % 2
    y = r // 8
    row0 = r - x
    z = t // 2
    core = t % 2
    sib = (r, t + 1 - 2 * core)

    barrier = pltpu.get_barrier_semaphore()

    def greet_rep(i, carry):
        pl.semaphore_signal(
            barrier, inc=1, device_id=((r + i) % REP, t), device_id_type=MESH
        )
        return carry

    lax.fori_loop(1, REP, greet_rep, 0)

    def greet_row(i, carry):
        peer = (row0 + (x + i // 3) % 4, ((z + 1 + i % 3) % 4) * 2 + core)
        pl.semaphore_signal(barrier, inc=1, device_id=peer, device_id_type=MESH)
        return carry

    lax.fori_loop(0, 12, greet_row, 0)
    pl.semaphore_signal(barrier, inc=1, device_id=sib, device_id_type=MESH)

    k_load = pltpu.make_async_copy(k_hbm, kbuf, load_sem.at[0])
    v_load = pltpu.make_async_copy(v_hbm, vbuf, load_sem.at[1])
    ad_load = pltpu.make_async_copy(adown_hbm, adown, load_sem.at[2])
    w_load = pltpu.make_async_copy(w_hbm, wbuf, load_sem.at[3])
    au_load = pltpu.make_async_copy(aup_hbm, aup, load_sem.at[4])
    for copy in (k_load, v_load, ad_load, w_load, au_load):
        copy.start()

    queries = q_ref[...]
    q_heads = jnp.concatenate(
        [queries[:, h * HD : (h + 1) * HD] for h in range(HEADS)], axis=0
    )
    new_keys = nk_ref[...]
    new_values = nv_ref[...]
    stacked = jnp.concatenate([q_heads, new_keys, new_values], axis=0)
    line = iota((64, 192), 0)
    place = line % 16
    col = iota((64, 192), 1)
    kind = jnp.where(
        place < 8,
        place % 4,
        jnp.where(place < 10, 4, jnp.where(place < 12, 5, 9)),
    )
    within = jnp.where(place < 8, place // 4, place % 2)
    entry = (line // 16) * CAP + within
    wanted = jnp.full((64, 192), -1, jnp.int32)
    for j in range(SPAN * CAP):
        wanted = jnp.where(entry == j, recv_s[0, j], wanted)
    pick = (kind == col // REQ) & (wanted == col % REQ)
    gathered = dot(pick.astype(BF16), stacked).astype(BF16)
    for g in range(SPAN):
        qout[g] = gathered[g * 16 : (g + 1) * 16]

    lane1 = iota((1, 128), 1)
    recv4 = jnp.full((1, 128), -1, jnp.int32)
    for j in range(SPAN * CAP):
        recv4 = jnp.where(lane1 // 4 == j, recv_s[0, j], recv4)
    slots = slot_row[...]
    target = jnp.full((1, REQ), -1, jnp.int32)
    for k in range(SLOTS):
        target = jnp.where(slots == k, install_s[0, k], target)
    target = jnp.concatenate([target, jnp.full((1, 128 - REQ), -1, jnp.int32)], axis=1)
    sub8 = iota((8, 128), 0)
    meta[x] = jnp.where(sub8 == 0, recv4, jnp.where(sub8 == 1, target, -1))

    pl.semaphore_wait(barrier, 31 + 12 + 1)

    sends = []

    q_copies = []
    for g, distance in enumerate(DISTANCES):
        copy = remote(
            qout.at[g],
            qin.at[g],
            q_ssem.at[g],
            q_rsem.at[g],
            ((r + REP - distance) % REP, t),
        )
        copy.start()
        q_copies.append(copy)
    sends += q_copies

    my_dn = pl.ds(pl.multiple_of(r * RANK_PART, RANK_PART), RANK_PART)
    my_up = pl.ds(pl.multiple_of(r * RANK, RANK), RANK)

    def dn_part(c):
        return sdown_hbm.at[pl.ds(pl.multiple_of(c * RANK_PART, RANK_PART), RANK_PART)]

    def up_part(c):
        return sup_hbm.at[:, pl.ds(pl.multiple_of(c * OUT_PART, OUT_PART), OUT_PART)]

    own_dn = pltpu.make_async_copy(dn_part(x), sdn.at[my_dn], s1_local.at[0])
    own_up = pltpu.make_async_copy(up_part(x), sup.at[my_up], s1_local.at[1])
    own_dn.start()
    own_up.start()
    near_dn, near_up, far_dn, far_up = [], [], [], []
    for o in range(1, 4):
        c = (x + o) % 4
        near_dn.append(
            remote(dn_part(c), sdn.at[my_dn], s1_ssem.at[0, o], s1_rsem.at[0, o], (row0 + c, t))
        )
        near_up.append(
            remote(up_part(c), sup.at[my_up], s1_ssem.at[1, o], s1_rsem.at[1, o], (row0 + c, t))
        )
    other0 = y * 8 + (1 - zh) * 4
    for o in range(4):
        c = (x + o) % 4
        far_dn.append(
            remote(dn_part(c), sdn.at[my_dn], s1_ssem.at[2, o], s1_rsem.at[2, o], (other0 + c, t))
        )
        far_up.append(
            remote(up_part(c), sup.at[my_up], s1_ssem.at[3, o], s1_rsem.at[3, o], (other0 + c, t))
        )
    for copy in far_dn + near_dn + near_up + far_up:
        copy.start()
    sends += near_dn + near_up + far_dn + far_up

    meta_copies = []
    for o in range(1, 4):
        copy = remote(
            meta.at[x], meta.at[x], meta_ssem.at[o], meta_rsem.at[o], (row0 + (x + o) % 4, t)
        )
        copy.start()
        meta_copies.append(copy)
    sends += meta_copies

    def stage2(half, tag):
        first = y * 8 + half * 4
        dn_rows = pl.ds(pl.multiple_of(first * RANK_PART, 4 * RANK_PART), 4 * RANK_PART)
        up_rows = pl.ds(pl.multiple_of(first * RANK, 4 * RANK), 4 * RANK)
        dn, up = [], []
        for o in range(1, 4):
            peer = ((r + 8 * o) % REP, t)
            dn.append(
                remote(
                    sdn.at[dn_rows], sdn.at[dn_rows], s2_ssem.at[tag, o], s2_rsem.at[tag, o], peer
                )
            )
            up.append(
                remote(
                    sup.at[up_rows],
                    sup.at[up_rows],
                    s2_ssem.at[2 + tag, o],
                    s2_rsem.at[2 + tag, o],
                    peer,
                )
            )
        return dn, up

    s2_near_dn, s2_near_up = stage2(zh, 0)
    s2_far_dn, s2_far_up = stage2(1 - zh, 1)
    sends += s2_near_dn + s2_near_up + s2_far_dn + s2_far_up

    fc = iota((5 * 512, 128), 0)
    fl = iota((5 * 512, 128), 1)
    block = fc // 512
    goal = jnp.where(block < 4, block * RANK_PART + fc % RANK_PART, 64 + fc % RANK)
    fold[...] = (fl == goal).astype(BF16)
    pc = iota((512, 512), 0)
    pj = iota((512, 512), 1)
    inner = pc % 128
    hit = (
        (inner < 64)
        & (inner // RANK_PART == pj // 128)
        & (pj % 64 == (pc // 128) * RANK_PART + pc % RANK_PART)
    )
    perm[...] = hit.astype(BF16)

    own_dn.wait()
    k_load.wait()
    er = iota((256, 128), 0)
    ec = iota((256, 128), 1)
    spread_q = ((er % 8 == ec // REQ) & (er // 8 == ec % REQ)).astype(BF16)
    q_local = dot(spread_q, q_heads)
    spread_r = iota((256, REQ), 0) // 8 == iota((256, REQ), 1)
    new_kv = dot(spread_r.astype(BF16), jnp.concatenate([new_keys, new_values], axis=1))
    lengths = jnp.sum(
        jnp.where(spread_r, len_row[...], 0).astype(F32), axis=1, keepdims=True
    ).astype(jnp.int32)
    scores = lax.dot_general(
        q_local.reshape(REQ, 8, HD).astype(BF16),
        kbuf[...],
        (((2,), (2,)), ((0,), (0,))),
        preferred_element_type=F32,
    ).reshape(256, LMAX)
    own = jnp.sum(q_local * new_kv[:, :HD], axis=1, keepdims=True)
    weights, own_b, total = softmax_parts(scores, own, ec < lengths)
    v_load.wait()
    summed = lax.dot_general(
        weights.reshape(REQ, 8, LMAX),
        vbuf[...],
        (((2,), (1,)), ((0,), (0,))),
        preferred_element_type=F32,
    ).reshape(256, HD)
    obuf[...] = (summed + own_b * new_kv[:, HD:]) / total
    for h in range(HEADS):
        loc[x, :, h * HD : (h + 1) * HD] = obuf[pl.ds(h, REQ, stride=8), :].astype(BF16)

    loc_copies = []
    for o in range(1, 4):
        copy = remote(
            loc.at[x], loc.at[x], loc_ssem.at[o], loc_rsem.at[o], (row0 + (x + o) % 4, t)
        )
        copy.start()
        loc_copies.append(copy)
    sends += loc_copies

    for copy in q_copies:
        copy.wait_recv()
    head8 = iota((8, HD), 0) // HEADS == 0
    line32 = iota((32, 128), 0) // HEADS
    moved_len = jnp.zeros((32, 128), jnp.int32)
    moved_scores, moved_own, moved_values, places = [], [], [], []
    for g in range(SPAN):
        arrived = qin[g]
        arrived_f = arrived.astype(F32)
        q8 = arrived[0:8]
        parts = []
        for i in range(CAP):
            j = g * CAP + i
            at = jnp.maximum(send_s[0, j], 0)
            places.append(at)
            parts.append(dot_nt(q8, kbuf[at]))
            moved_len = jnp.where(line32 == j, len_s[0, at], moved_len)
        moved_scores.append(jnp.where(head8, parts[0], parts[1]))
        key = jnp.where(head8, arrived_f[8:9], arrived_f[9:10])
        moved_own.append(jnp.sum(arrived_f[0:8] * key, axis=1, keepdims=True))
        moved_values.append(jnp.where(head8, arrived_f[10:11], arrived_f[11:12]))
    m_weights, m_own, m_total = softmax_parts(
        jnp.concatenate(moved_scores, axis=0),
        jnp.concatenate(moved_own, axis=0),
        iota((32, 128), 1) < moved_len,
    )
    m_summed = []
    m_wf = m_weights.astype(F32)
    for g in range(SPAN):
        w8 = m_wf[g * 8 : (g + 1) * 8].astype(BF16)
        a = dot(w8, vbuf[places[g * CAP]])
        b = dot(w8, vbuf[places[g * CAP + 1]])
        m_summed.append(jnp.where(head8, a, b))
    m_out = (
        jnp.concatenate(m_summed, axis=0) + m_own * jnp.concatenate(moved_values, axis=0)
    ) / m_total
    m_out = m_out.astype(BF16).astype(F32)
    for g in range(SPAN):
        res[g] = m_out[g * 8 : (g + 1) * 8]

    mig_sends = []
    for g, distance in enumerate(DISTANCES):
        home = (r + distance) % REP
        home_x = home % 4
        for c in range(ROW):
            device = home - home_x + c
            dst = mig.at[home_x, pl.ds(8 * g, 8)]
            copy = remote(
                res.at[g], dst, mig_ssem.at[g, c], mig_rsem.at[home_x, g], (device, t)
            )
            if g == 0:
                here = pltpu.make_async_copy(res.at[g], dst, mig_rsem.at[home_x, g])

                @pl.when(device == r)
                def _():
                    here.start()

                @pl.when(device != r)
                def _():
                    copy.start()

                mig_sends.append((copy, device))
            else:
                copy.start()
                sends.append(copy)

    for copy in near_dn:
        copy.wait_recv()
    for copy in s2_near_dn:
        copy.start()
    for copy in far_dn:
        copy.wait_recv()
    for copy in s2_far_dn:
        copy.start()
    own_up.wait()
    for copy in near_up:
        copy.wait_recv()
    for copy in s2_near_up:
        copy.start()

    for copy in meta_copies:
        copy.wait_recv()
    for copy in loc_copies:
        copy.wait_recv()
    for h in range(ROW):
        for g in range(SPAN):
            remote(res.at[0], mig.at[h, pl.ds(8 * g, 8)], mig_ssem.at[g, 0], mig_rsem.at[h, g], sib).wait_recv()
    mh = iota((128, 32), 0)
    ml = iota((128, 32), 1)
    tcols = []
    for h in range(ROW):
        tile = meta[h]
        tcols.append(to_column(tile[1:2], REQ))
        recv_row = tile[0:1, 0:32]
        put = ((mh % REQ == recv_row) & (mh // REQ == ml % 4)).astype(BF16)
        rows = dot(put, mig[h].astype(BF16)).astype(BF16)
        taken = jnp.max(
            jnp.where(iota((REQ, 32), 0) == recv_row, 1.0, 0.0), axis=1, keepdims=True
        )
        here = loc[h]
        for k in range(HEADS):
            span = slice(k * HD, (k + 1) * HD)
            merged[h * REQ : (h + 1) * REQ, span] = jnp.where(
                taken > 0.5, rows[k * REQ : (k + 1) * REQ], here[:, span]
            )

    mine = merged[pl.ds(pl.multiple_of(x * REQ, REQ), REQ), :]

    w_load.wait()

    def project(zq, cq):
        first = pl.multiple_of((zq * 2 + cq) * OUT, OUT)
        return dot_nt(mine, wbuf[pl.ds(first, OUT), :])

    sib_copies = []
    rs_copies = []
    order = (2, 1, 3, 0)

    def opposite(n):
        zq = (z + order[n]) % 4
        sib_out[n] = project(zq, 1 - core).astype(BF16)
        copy = remote(sib_out.at[n], sib_in.at[n], sib_ssem.at[n], sib_rsem.at[n], sib)
        copy.start()
        sib_copies.append(copy)

    def same(n):
        rs_own[n] = project((z + order[n]) % 4, core)

    def pass_on(n):
        zq = (z + order[n]) % 4
        sib_copies[n].wait_recv()
        both = rs_own[n] + sib_in[n].astype(F32)
        if order[n] == 0:
            rs_own[n] = both
            return
        rs_out[n] = both.astype(BF16)
        copy = remote(
            rs_out.at[n], rs_in.at[n], rs_ssem.at[n], rs_rsem.at[n], (r, zq * 2 + core)
        )
        copy.start()
        rs_copies.append(copy)

    opposite(0)
    same(0)
    opposite(1)
    pass_on(0)
    same(1)

    ad_load.wait()
    slot_col = to_column(
        jnp.concatenate([slots, jnp.full((1, 128 - REQ), -1, jnp.int32)], axis=1), REQ
    )
    target_col = to_column(meta[x][1:2], REQ)
    resident = target_col < 0
    c512 = iota((REQ, 512), 1)
    part = dot_nt(mine, adown[...])
    pieces = [jnp.where((c512 // RANK == slot_col) & resident, part, 0.0)]
    for copy in s2_near_dn + s2_far_dn:
        copy.wait_recv()
    part = dot_nt(merged[...], sdn[...])
    sections = [
        jnp.where(c512 // RANK_PART == tcols[h], part[h * REQ : (h + 1) * REQ], 0.0)
        for h in range(ROW)
    ]
    masked = jnp.concatenate(sections + pieces, axis=1).astype(BF16)
    msg[0] = dot(masked, fold[...]).astype(BF16)
    msg_copy = remote(msg.at[0], msg_sib, msg_sem.at[0], msg_sem.at[1], sib)
    msg_copy.start()
    for copy in far_up:
        copy.wait_recv()
    for copy in s2_far_up:
        copy.start()
    opposite(2)
    pass_on(1)
    msg_copy.wait_recv()
    bc[x, z] = (msg[0].astype(F32) + msg_sib[...].astype(F32)).astype(BF16)
    bc_copies = []
    for xo in range(4):
        for zo in range(4):
            if xo == 0 and zo == 0:
                continue
            copy = remote(
                bc.at[x, z],
                bc.at[x, z],
                bc_ssem.at[xo, zo],
                bc_rsem.at[xo, zo],
                (row0 + (x + xo) % 4, ((z + zo) % 4) * 2 + core),
            )
            copy.start()
            bc_copies.append(copy)
    sends += bc_copies
    same(2)
    opposite(3)
    pass_on(2)
    same(3)
    pass_on(3)

    for copy in bc_copies:
        copy.wait_recv()
    sums = []
    for h in range(ROW):
        sums.append(
            (bc[h, 0].astype(F32) + bc[h, 1].astype(F32))
            + (bc[h, 2].astype(F32) + bc[h, 3].astype(F32))
        )
    shrunk = dot(jnp.concatenate(sums, axis=1).astype(BF16), perm[...])
    lane = iota((REQ, 128), 1)
    for h in range(ROW):
        ranks = shrunk[:, h * 128 : (h + 1) * 128]
        for n in range(16):
            sexp[h * REQ : (h + 1) * REQ, n * 128 : (n + 1) * 128] = jnp.where(
                lane // RANK + 2 * n == tcols[h], ranks, 0.0
            ).astype(BF16)
    for copy in s2_near_up + s2_far_up:
        copy.wait_recv()
    delta = dot(sexp[...], sup[...])
    dlt_copies = []
    for h in range(ROW):
        dlt_out[h] = delta[h * REQ : (h + 1) * REQ].astype(BF16)
    dlt_in[x] = dlt_out[x]
    for o in range(1, 4):
        c = (x + o) % 4
        copy = remote(
            dlt_out.at[c], dlt_in.at[x], dlt_ssem.at[o], dlt_rsem.at[o], (row0 + c, t)
        )
        copy.start()
        dlt_copies.append(copy)
    sends += dlt_copies

    au_load.wait()
    own_sum = (bc[x, 0].astype(F32) + bc[x, 1].astype(F32)) + (
        bc[x, 2].astype(F32) + bc[x, 3].astype(F32)
    )
    ranks = jnp.where(lane < RANK, pltpu.roll(own_sum, RANK, 1), own_sum)
    spread = jnp.concatenate(
        [
            jnp.where((lane // RANK + 2 * n == slot_col) & resident, ranks, 0.0)
            for n in range(SLOTS // 2)
        ],
        axis=1,
    ).astype(BF16)
    acc = dot(spread, aup[...]) + rs_own[3]

    for copy in rs_copies:
        copy.wait_recv()
    for n in range(3):
        acc = acc + rs_in[n].astype(F32)
    for copy in dlt_copies:
        copy.wait_recv()
    out_ref[...] = (
        acc + jnp.concatenate([dlt_in[h].astype(F32) for h in range(ROW)], axis=1)
    ).astype(BF16)

    msg_copy.wait_send()
    for copy in sib_copies + rs_copies + sends:
        copy.wait_send()
    for copy, device in mig_sends:

        @pl.when(device != r)
        def _():
            copy.wait_send()


def body(
    queries,
    k_cache,
    v_cache,
    new_keys,
    new_values,
    kv_len,
    send_rows,
    recv_rows,
    out_weight,
    adapter_down,
    adapter_up,
    sectioned_down,
    sectioned_up,
    install,
    adapter_slot,
):
    vmem = pl.BlockSpec(memory_space=pltpu.VMEM)
    smem = pl.BlockSpec(memory_space=pltpu.SMEM)
    hbm = pl.BlockSpec(memory_space=pl.ANY)
    dma = pltpu.SemaphoreType.DMA
    lengths = kv_len.reshape(1, REQ)
    return pl.pallas_call(
        kernel,
        out_shape=jax.ShapeDtypeStruct((REQ, OUT), BF16),
        in_specs=[vmem, hbm, hbm, vmem, vmem, vmem, vmem, smem, smem, smem, smem]
        + [hbm] * 5,
        out_specs=vmem,
        scratch_shapes=[
            pltpu.VMEM((REQ, LMAX, HD), BF16),
            pltpu.VMEM((REQ, LMAX, HD), BF16),
            pltpu.VMEM((TP * OUT, QW), BF16),
            pltpu.VMEM((SLOTS * RANK, QW), BF16),
            pltpu.VMEM((SLOTS * RANK, OUT), BF16),
            pltpu.VMEM((REP * RANK_PART, QW), BF16),
            pltpu.VMEM((REP * RANK, OUT_PART), BF16),
            pltpu.VMEM((SPAN, 16, HD), BF16),
            pltpu.VMEM((SPAN, 16, HD), BF16),
            pltpu.VMEM((ROW, 8, 128), jnp.int32),
            pltpu.VMEM((SPAN, 8, HD), F32),
            pltpu.VMEM((ROW, 32, HD), F32),
            pltpu.VMEM((ROW, REQ, QW), BF16),
            pltpu.VMEM((ROW * REQ, QW), BF16),
            pltpu.VMEM((256, HD), F32),
            pltpu.VMEM((5 * 512, 128), BF16),
            pltpu.VMEM((512, 512), BF16),
            pltpu.VMEM((1, REQ, 128), BF16),
            pltpu.VMEM((REQ, 128), BF16),
            pltpu.VMEM((4, 4, REQ, 128), BF16),
            pltpu.VMEM((ROW * REQ, REP * RANK), BF16),
            pltpu.VMEM((ROW, REQ, OUT_PART), BF16),
            pltpu.VMEM((ROW, REQ, OUT_PART), BF16),
            pltpu.VMEM((4, REQ, OUT), BF16),
            pltpu.VMEM((4, REQ, OUT), BF16),
            pltpu.VMEM((4, REQ, OUT), F32),
            pltpu.VMEM((3, REQ, OUT), BF16),
            pltpu.VMEM((3, REQ, OUT), BF16),
            dma((5,)),
            dma((2,)),
            dma((4, 4)),
            dma((4, 4)),
            dma((4, 4)),
            dma((4, 4)),
            dma((4,)),
            dma((4,)),
            dma((4,)),
            dma((4,)),
            dma((4, 4)),
            dma((4, 4)),
            dma((4,)),
            dma((4,)),
            dma((2,)),
            dma((4, 4)),
            dma((4, 4)),
            dma((4,)),
            dma((4,)),
            dma((4,)),
            dma((4,)),
            dma((4,)),
            dma((4,)),
        ],
        compiler_params=pltpu.CompilerParams(
            collective_id=0, has_side_effects=True, vmem_limit_bytes=48 << 20
        ),
    )(
        queries,
        k_cache,
        v_cache,
        new_keys,
        new_values,
        lengths,
        adapter_slot.reshape(1, REQ),
        lengths,
        send_rows,
        recv_rows,
        install,
        out_weight,
        adapter_down.reshape(SLOTS * RANK, QW),
        adapter_up.reshape(SLOTS * RANK, OUT),
        sectioned_down.reshape(RANK, QW),
        sectioned_up.reshape(RANK, OUT),
    )


def solution(mesh):
    placed = (
        P("rep", "tp"),
        P("rep", None, "tp"),
        P("rep", None, "tp"),
        P("rep", "tp"),
        P("rep", "tp"),
        P("rep"),
        P("rep", None),
        P("rep", None),
        P(None, "tp"),
        P("rep", None, "tp"),
        P("rep", None, "tp"),
        P("rep", None, "tp"),
        P("rep", None, "tp"),
        P("rep", None),
        P("rep"),
    )
    return jax.shard_map(
        body, mesh=mesh, in_specs=placed, out_specs=P("rep", "tp"), check_vma=False
    )
```

```python
import functools

import jax
import jax.numpy as jnp
from jax import lax
from jax.experimental import pallas as pl
from jax.experimental.pallas import tpu as pltpu
from jax.sharding import PartitionSpec as P

MESH = pl.DeviceIdType.MESH
F32 = jnp.float32
BF16 = jnp.bfloat16

HD = 128
HEADS = 4
REQ = 32
LMAX = 128
RANK = 64
SLOTS = 8
SPAN = 4
CAP = 2
REP = 32
TP = 8
ROW = 4
QW = HEADS * HD
OUT = 1024
RANK_PART = RANK // ROW
OUT_PART = OUT // ROW
SCALE = HD**-0.5
DISTANCES = (1, 8, 12, 16)
FAR_FIRST = (2, 0, 3, 1)


def iota(shape, dim):
    return lax.broadcasted_iota(jnp.int32, shape, dim)


def dot(a, b):
    return lax.dot_general(a, b, (((1,), (0,)), ((), ())), preferred_element_type=F32)


def dot_nt(a, b):
    return lax.dot_general(a, b, (((1,), (1,)), ((), ())), preferred_element_type=F32)


def remote(src, dst, ssem, rsem, device):
    return pltpu.make_async_remote_copy(
        src_ref=src,
        dst_ref=dst,
        send_sem=ssem,
        recv_sem=rsem,
        device_id=device,
        device_id_type=MESH,
    )


def softmax_parts(scores, own, live):
    scores = jnp.where(live, scores * SCALE, -jnp.inf)
    own = own * SCALE
    top = jnp.maximum(jnp.max(scores, axis=1, keepdims=True), own)
    weights = jnp.exp(scores - top)
    own_weight = jnp.exp(own - top)
    total = jnp.sum(weights, axis=1, keepdims=True) + own_weight
    return weights.astype(BF16), own_weight.astype(BF16).astype(F32), total


def to_column(row, rows):
    spread = jnp.where(iota((rows, 128), 0) == iota((rows, 128), 1), row, 0)
    return jnp.sum(spread.astype(F32), axis=1, keepdims=True).astype(jnp.int32)


def kernel(
    q_hbm,
    k_hbm,
    v_hbm,
    nk_hbm,
    nv_hbm,
    len_hbm,
    slot_hbm,
    send_hbm,
    recv_hbm,
    install_hbm,
    w_hbm,
    adown_hbm,
    aup_hbm,
    sdown_hbm,
    sup_hbm,
    out_ref,
    q_ref,
    nk_ref,
    nv_ref,
    len_row,
    slot_row,
    len_s,
    send_s,
    recv_s,
    install_s,
    kbuf,
    vbuf,
    wbuf,
    adown,
    aup,
    sdn,
    sup,
    qout,
    qin,
    meta,
    res,
    mig,
    merged,
    obuf,
    fold,
    perm,
    msg,
    msg_sib,
    bc,
    sexp,
    dlt_out,
    dlt_in,
    sib_out,
    sib_in,
    rs_own,
    rs_out,
    rs_in,
    small_sem,
    load_sem,
    s1_local,
    s1_ssem,
    s1_rsem,
    s2_ssem,
    s2_rsem,
    q_ssem,
    q_rsem,
    meta_ssem,
    meta_rsem,
    mig_ssem,
    mig_rsem,
    loc_ssem,
    loc_rsem,
    msg_sem,
    bc_ssem,
    bc_rsem,
    dlt_ssem,
    dlt_rsem,
    sib_ssem,
    sib_rsem,
    rs_ssem,
    rs_rsem,
):
    r = lax.axis_index("rep")
    t = lax.axis_index("tp")
    x = r % 4
    zh = (r // 4) % 2
    y = r // 8
    row0 = r - x
    z = t // 2
    core = t % 2
    sib = (r, t + 1 - 2 * core)

    other0 = y * 8 + (1 - zh) * 4
    greeted = [((r + o) % REP, t) for o in (12, 20)]
    greeted += [(other0 + (x + o) % 4, t) for o in (2, 1, 3, 0)]
    greeted += [((r + o) % REP, t) for o in (1, 31, 16, 8, 24)]
    greeted += [
        (row0 + (x + xo) % 4, ((z + zo) % 4) * 2 + core)
        for xo in (2, 1, 3, 0)
        for zo in (2, 1, 3, 0)
        if xo or zo
    ]
    greeted.append(sib)
    barrier = pltpu.get_barrier_semaphore()
    for peer in greeted:
        pl.semaphore_signal(barrier, inc=1, device_id=peer, device_id_type=MESH)

    small = [
        pltpu.make_async_copy(src, dst, small_sem.at[n])
        for n, (src, dst) in enumerate(
            (
                (q_hbm, q_ref),
                (nk_hbm, nk_ref),
                (nv_hbm, nv_ref),
                (recv_hbm, recv_s),
                (install_hbm, install_s),
                (slot_hbm, slot_row),
                (len_hbm, len_row),
                (len_hbm, len_s),
                (send_hbm, send_s),
            )
        )
    ]
    for copy in small:
        copy.start()
    k_load = pltpu.make_async_copy(k_hbm, kbuf, load_sem.at[0])
    v_load = pltpu.make_async_copy(v_hbm, vbuf, load_sem.at[1])
    ad_load = pltpu.make_async_copy(adown_hbm, adown, load_sem.at[2])
    w_load = pltpu.make_async_copy(w_hbm, wbuf, load_sem.at[3])
    au_load = pltpu.make_async_copy(aup_hbm, aup, load_sem.at[4])
    for copy in (k_load, v_load, ad_load, w_load, au_load):
        copy.start()
    for copy in small:
        copy.wait()

    queries = q_ref[...]
    q_heads = jnp.concatenate(
        [queries[:, h * HD : (h + 1) * HD] for h in range(HEADS)], axis=0
    )
    new_keys = nk_ref[...]
    new_values = nv_ref[...]
    stacked = jnp.concatenate([q_heads, new_keys, new_values], axis=0)
    line = iota((64, 192), 0)
    place = line % 16
    col = iota((64, 192), 1)
    kind = jnp.where(
        place < 8,
        place % 4,
        jnp.where(place < 10, 4, jnp.where(place < 12, 5, 9)),
    )
    within = jnp.where(place < 8, place // 4, place % 2)
    entry = (line // 16) * CAP + within
    wanted = jnp.full((64, 192), -1, jnp.int32)
    for j in range(SPAN * CAP):
        wanted = jnp.where(entry == j, recv_s[0, j], wanted)
    pick = (kind == col // REQ) & (wanted == col % REQ)
    gathered = dot(pick.astype(BF16), stacked).astype(BF16)
    for g in range(SPAN):
        qout[g] = gathered[g * 16 : (g + 1) * 16]

    lane1 = iota((1, 128), 1)
    recv4 = jnp.full((1, 128), -1, jnp.int32)
    for j in range(SPAN * CAP):
        recv4 = jnp.where(lane1 // 4 == j, recv_s[0, j], recv4)
    slots = slot_row[...]
    target = jnp.full((1, REQ), -1, jnp.int32)
    for k in range(SLOTS):
        target = jnp.where(slots == k, install_s[0, k], target)
    target = jnp.concatenate([target, jnp.full((1, 128 - REQ), -1, jnp.int32)], axis=1)
    sub8 = iota((8, 128), 0)
    meta[x] = jnp.where(sub8 == 1, target, -1)

    k_load.wait()
    er = iota((256, 128), 0)
    ec = iota((256, 128), 1)
    spread_q = ((er % 8 == ec // REQ) & (er // 8 == ec % REQ)).astype(BF16)
    q_local = dot(spread_q, q_heads)
    spread_r = iota((256, REQ), 0) // 8 == iota((256, REQ), 1)
    new_kv = dot(spread_r.astype(BF16), jnp.concatenate([new_keys, new_values], axis=1))
    lengths = jnp.sum(
        jnp.where(spread_r, len_row[...], 0).astype(F32), axis=1, keepdims=True
    ).astype(jnp.int32)
    scores = lax.dot_general(
        q_local.reshape(REQ, 8, HD).astype(BF16),
        kbuf[...],
        (((2,), (2,)), ((0,), (0,))),
        preferred_element_type=F32,
    ).reshape(256, LMAX)
    own = jnp.sum(q_local * new_kv[:, :HD], axis=1, keepdims=True)
    weights, own_b, total = softmax_parts(scores, own, ec < lengths)
    v_load.wait()
    summed = lax.dot_general(
        weights.reshape(REQ, 8, LMAX),
        vbuf[...],
        (((2,), (1,)), ((0,), (0,))),
        preferred_element_type=F32,
    ).reshape(256, HD)
    obuf[...] = (summed + own_b * new_kv[:, HD:]) / total
    here = jnp.concatenate(
        [obuf[pl.ds(h, REQ, stride=8), :] for h in range(HEADS)], axis=1
    ).astype(BF16)

    fc = iota((5 * 512, 128), 0)
    fl = iota((5 * 512, 128), 1)
    block = fc // 512
    goal = jnp.where(block < 4, block * RANK_PART + fc % RANK_PART, 64 + fc % RANK)
    fold[...] = (fl == goal).astype(BF16)
    pc = iota((512, 512), 0)
    pj = iota((512, 512), 1)
    inner = pc % 128
    hit = (
        (inner < 64)
        & (inner // RANK_PART == pj // 128)
        & (pj % 64 == (pc // 128) * RANK_PART + pc % RANK_PART)
    )
    perm[...] = hit.astype(BF16)

    pl.semaphore_wait(barrier, len(greeted))

    sends = []

    q_copies = []
    for g in FAR_FIRST:
        copy = remote(
            qout.at[g],
            qin.at[g],
            q_ssem.at[g],
            q_rsem.at[g],
            ((r + REP - DISTANCES[g]) % REP, t),
        )
        copy.start()
        q_copies.append(copy)
    sends += q_copies

    my_dn = pl.ds(pl.multiple_of(r * RANK_PART, RANK_PART), RANK_PART)
    my_up = pl.ds(pl.multiple_of(r * RANK, RANK), RANK)

    def dn_part(c):
        return sdown_hbm.at[pl.ds(pl.multiple_of(c * RANK_PART, RANK_PART), RANK_PART)]

    def up_part(c):
        return sup_hbm.at[:, pl.ds(pl.multiple_of(c * OUT_PART, OUT_PART), OUT_PART)]

    own_dn = pltpu.make_async_copy(dn_part(x), sdn.at[my_dn], s1_local.at[0])
    own_up = pltpu.make_async_copy(up_part(x), sup.at[my_up], s1_local.at[1])
    own_dn.start()
    own_up.start()
    near_dn, near_up, far_dn, far_up = [], [], [], []
    for o in range(1, 4):
        c = (x + o) % 4
        near_dn.append(
            remote(dn_part(c), sdn.at[my_dn], s1_ssem.at[0, o], s1_rsem.at[0, o], (row0 + c, t))
        )
        near_up.append(
            remote(up_part(c), sup.at[my_up], s1_ssem.at[1, o], s1_rsem.at[1, o], (row0 + c, t))
        )
    for o in range(4):
        c = (x + o) % 4
        far_dn.append(
            remote(dn_part(c), sdn.at[my_dn], s1_ssem.at[2, o], s1_rsem.at[2, o], (other0 + c, t))
        )
        far_up.append(
            remote(up_part(c), sup.at[my_up], s1_ssem.at[3, o], s1_rsem.at[3, o], (other0 + c, t))
        )
    for copy in far_dn + near_dn + near_up + far_up:
        copy.start()
    sends += near_dn + near_up + far_dn + far_up

    meta_copies = []
    for o in range(1, 4):
        copy = remote(
            meta.at[x], meta.at[x], meta_ssem.at[o], meta_rsem.at[o], (row0 + (x + o) % 4, t)
        )
        copy.start()
        meta_copies.append(copy)
    sends += meta_copies

    def stage2(half, tag):
        first = y * 8 + half * 4
        dn_rows = pl.ds(pl.multiple_of(first * RANK_PART, 4 * RANK_PART), 4 * RANK_PART)
        up_rows = pl.ds(pl.multiple_of(first * RANK, 4 * RANK), 4 * RANK)
        dn, up = [], []
        for o in range(1, 4):
            peer = ((r + 8 * o) % REP, t)
            dn.append(
                remote(
                    sdn.at[dn_rows], sdn.at[dn_rows], s2_ssem.at[tag, o], s2_rsem.at[tag, o], peer
                )
            )
            up.append(
                remote(
                    sup.at[up_rows],
                    sup.at[up_rows],
                    s2_ssem.at[2 + tag, o],
                    s2_rsem.at[2 + tag, o],
                    peer,
                )
            )
        return dn, up

    s2_near_dn, s2_near_up = stage2(zh, 0)
    s2_far_dn, s2_far_up = stage2(1 - zh, 1)
    sends += s2_near_dn + s2_near_up + s2_far_dn + s2_far_up

    order = (2, 1, 3, 0)

    class Wave:
        def __init__(self, rows, own, sib_out, sib_in, out, arriving, sems):
            self.rows, self.own, self.out, self.arriving = rows, own, out, arriving
            self.sib_out, self.sib_in, self.sems = sib_out, sib_in, sems
            self.sib_copies, self.copies = [], []

        def project(self, zq, cq):
            first = pl.multiple_of((zq * 2 + cq) * OUT, OUT)
            return dot_nt(self.rows, wbuf[pl.ds(first, OUT), :])

        def opposite(self, n):
            self.sib_out[n] = self.project((z + order[n]) % 4, 1 - core).astype(BF16)
            copy = remote(
                self.sib_out.at[n], self.sib_in.at[n], self.sems[0].at[n], self.sems[1].at[n], sib
            )
            copy.start()
            self.sib_copies.append(copy)

        def same(self, n):
            self.own[n] = self.project((z + order[n]) % 4, core)

        def pass_on(self, n):
            zq = (z + order[n]) % 4
            self.sib_copies[n].wait_recv()
            both = self.own[n] + self.sib_in[n].astype(F32)
            if order[n] == 0:
                self.own[n] = both
                return
            self.out[n] = both.astype(BF16)
            copy = remote(
                self.out.at[n],
                self.arriving.at[n],
                self.sems[2].at[n],
                self.sems[3].at[n],
                (r, zq * 2 + core),
            )
            copy.start()
            self.copies.append(copy)

        def total(self):
            acc = self.own[3]
            for n, copy in enumerate(self.copies):
                copy.wait_recv()
                acc = acc + self.arriving[n].astype(F32)
            return acc

    own_dn.wait()
    for copy in near_dn:
        copy.wait_recv()
    for copy in s2_near_dn:
        copy.start()

    for copy in q_copies:
        copy.wait_recv()
    head8 = iota((8, HD), 0) // HEADS == 0
    line32 = iota((32, 128), 0) // HEADS
    moved_len = jnp.zeros((32, 128), jnp.int32)
    moved_scores, moved_own, moved_values, places = [], [], [], []
    for g in range(SPAN):
        arrived = qin[g]
        arrived_f = arrived.astype(F32)
        q8 = arrived[0:8]
        parts = []
        for i in range(CAP):
            j = g * CAP + i
            at = jnp.maximum(send_s[0, j], 0)
            places.append(at)
            parts.append(dot_nt(q8, kbuf[at]))
            moved_len = jnp.where(line32 == j, len_s[0, at], moved_len)
        moved_scores.append(jnp.where(head8, parts[0], parts[1]))
        key = jnp.where(head8, arrived_f[8:9], arrived_f[9:10])
        moved_own.append(jnp.sum(arrived_f[0:8] * key, axis=1, keepdims=True))
        moved_values.append(jnp.where(head8, arrived_f[10:11], arrived_f[11:12]))
    m_weights, m_own, m_total = softmax_parts(
        jnp.concatenate(moved_scores, axis=0),
        jnp.concatenate(moved_own, axis=0),
        iota((32, 128), 1) < moved_len,
    )
    m_summed = []
    m_wf = m_weights.astype(F32)
    for g in range(SPAN):
        w8 = m_wf[g * 8 : (g + 1) * 8].astype(BF16)
        a = dot(w8, vbuf[places[g * CAP]])
        b = dot(w8, vbuf[places[g * CAP + 1]])
        m_summed.append(jnp.where(head8, a, b))
    m_out = (
        jnp.concatenate(m_summed, axis=0) + m_own * jnp.concatenate(moved_values, axis=0)
    ) / m_total
    m_out = m_out.astype(BF16).astype(F32)
    for g in range(SPAN):
        res[g] = m_out[g * 8 : (g + 1) * 8]

    mig_copies = []
    for g in FAR_FIRST:
        copy = remote(
            res.at[g],
            mig.at[pl.ds(8 * g, 8)],
            mig_ssem.at[g],
            mig_rsem.at[g],
            ((r + DISTANCES[g]) % REP, t),
        )
        copy.start()
        mig_copies.append(copy)
    sends += mig_copies

    for copy in far_dn:
        copy.wait_recv()
    for copy in s2_far_dn:
        copy.start()
    own_up.wait()
    for copy in near_up:
        copy.wait_recv()
    for copy in s2_near_up:
        copy.start()

    for copy in mig_copies:
        copy.wait_recv()
    mh = iota((128, 32), 0)
    put = ((mh % REQ == recv4[:, 0:32]) & (mh // REQ == iota((128, 32), 1) % 4)).astype(BF16)
    rows = dot(put, mig[...].astype(BF16)).astype(BF16)
    taken = (
        jnp.max(
            jnp.where(iota((REQ, 32), 0) == recv4[:, 0:32], 1.0, 0.0), axis=1, keepdims=True
        )
        > 0.5
    )
    mine = jnp.where(
        taken,
        jnp.concatenate([rows[k * REQ : (k + 1) * REQ] for k in range(HEADS)], axis=1),
        here,
    )
    my_rows = pl.ds(pl.multiple_of(x * REQ, REQ), REQ)
    merged[my_rows, :] = mine
    row_copies = []
    for o in (2, 1, 3):
        copy = remote(
            merged.at[my_rows],
            merged.at[my_rows],
            loc_ssem.at[o],
            loc_rsem.at[o],
            (row0 + (x + o) % 4, t),
        )
        copy.start()
        row_copies.append(copy)
    sends += row_copies

    proj = Wave(
        mine, rs_own, sib_out, sib_in, rs_out, rs_in, (sib_ssem, sib_rsem, rs_ssem, rs_rsem)
    )
    w_load.wait()
    proj.opposite(0)
    proj.same(0)
    proj.opposite(1)
    proj.pass_on(0)

    ad_load.wait()
    slot_col = to_column(
        jnp.concatenate([slots, jnp.full((1, 128 - REQ), -1, jnp.int32)], axis=1), REQ
    )
    resident = to_column(target, REQ) < 0
    c512 = iota((REQ, 512), 1)
    part = dot_nt(mine, adown[...])
    pieces = [jnp.where((c512 // RANK == slot_col) & resident, part, 0.0)]
    for copy in meta_copies + row_copies + s2_near_dn + s2_far_dn:
        copy.wait_recv()
    tcols = [to_column(meta[h][1:2], REQ) for h in range(ROW)]
    part = dot_nt(merged[...], sdn[...])
    sections = [
        jnp.where(c512 // RANK_PART == tcols[h], part[h * REQ : (h + 1) * REQ], 0.0)
        for h in range(ROW)
    ]
    masked = jnp.concatenate(sections + pieces, axis=1).astype(BF16)
    msg[0] = dot(masked, fold[...]).astype(BF16)
    msg_copy = remote(msg.at[0], msg_sib, msg_sem.at[0], msg_sem.at[1], sib)
    msg_copy.start()
    for copy in far_up:
        copy.wait_recv()
    for copy in s2_far_up:
        copy.start()
    proj.same(1)
    proj.opposite(2)
    proj.pass_on(1)
    msg_copy.wait_recv()
    bc[x, z] = (msg[0].astype(F32) + msg_sib[...].astype(F32)).astype(BF16)
    bc_copies = []
    for xo in range(4):
        for zo in range(4):
            if xo == 0 and zo == 0:
                continue
            copy = remote(
                bc.at[x, z],
                bc.at[x, z],
                bc_ssem.at[xo, zo],
                bc_rsem.at[xo, zo],
                (row0 + (x + xo) % 4, ((z + zo) % 4) * 2 + core),
            )
            copy.start()
            bc_copies.append(copy)
    sends += bc_copies
    proj.same(2)
    proj.opposite(3)
    proj.pass_on(2)
    proj.same(3)
    proj.pass_on(3)

    for copy in bc_copies:
        copy.wait_recv()
    sums = []
    for h in range(ROW):
        sums.append(
            (bc[h, 0].astype(F32) + bc[h, 1].astype(F32))
            + (bc[h, 2].astype(F32) + bc[h, 3].astype(F32))
        )
    shrunk = dot(jnp.concatenate(sums, axis=1).astype(BF16), perm[...])
    lane = iota((REQ, 128), 1)
    for h in range(ROW):
        ranks = shrunk[:, h * 128 : (h + 1) * 128]
        for n in range(16):
            sexp[h * REQ : (h + 1) * REQ, n * 128 : (n + 1) * 128] = jnp.where(
                lane // RANK + 2 * n == tcols[h], ranks, 0.0
            ).astype(BF16)
    for copy in s2_near_up + s2_far_up:
        copy.wait_recv()
    delta = dot(sexp[...], sup[...])
    dlt_copies = []
    for h in range(ROW):
        dlt_out[h] = delta[h * REQ : (h + 1) * REQ].astype(BF16)
    dlt_in[x] = dlt_out[x]
    for o in range(1, 4):
        c = (x + o) % 4
        copy = remote(
            dlt_out.at[c], dlt_in.at[x], dlt_ssem.at[o], dlt_rsem.at[o], (row0 + c, t)
        )
        copy.start()
        dlt_copies.append(copy)
    sends += dlt_copies

    au_load.wait()
    own_sum = (bc[x, 0].astype(F32) + bc[x, 1].astype(F32)) + (
        bc[x, 2].astype(F32) + bc[x, 3].astype(F32)
    )
    ranks = jnp.where(lane < RANK, pltpu.roll(own_sum, RANK, 1), own_sum)
    spread = jnp.concatenate(
        [
            jnp.where((lane // RANK + 2 * n == slot_col) & resident, ranks, 0.0)
            for n in range(SLOTS // 2)
        ],
        axis=1,
    ).astype(BF16)
    acc = dot(spread, aup[...]) + proj.total()
    for copy in dlt_copies:
        copy.wait_recv()
    out_ref[...] = (
        acc + jnp.concatenate([dlt_in[h].astype(F32) for h in range(ROW)], axis=1)
    ).astype(BF16)

    msg_copy.wait_send()
    for copy in proj.sib_copies + proj.copies + sends:
        copy.wait_send()


def body(
    queries,
    k_cache,
    v_cache,
    new_keys,
    new_values,
    kv_len,
    send_rows,
    recv_rows,
    out_weight,
    adapter_down,
    adapter_up,
    sectioned_down,
    sectioned_up,
    install,
    adapter_slot,
):
    vmem = pl.BlockSpec(memory_space=pltpu.VMEM)
    hbm = pl.BlockSpec(memory_space=pltpu.HBM)
    smem = functools.partial(pltpu.SMEM, dtype=jnp.int32)
    dma = pltpu.SemaphoreType.DMA
    lengths = kv_len.reshape(1, REQ)
    return pl.pallas_call(
        kernel,
        out_shape=jax.ShapeDtypeStruct((REQ, OUT), BF16),
        in_specs=[hbm] * 15,
        out_specs=vmem,
        scratch_shapes=[
            pltpu.VMEM((REQ, QW), BF16),
            pltpu.VMEM((REQ, HD), BF16),
            pltpu.VMEM((REQ, HD), BF16),
            pltpu.VMEM((1, REQ), jnp.int32),
            pltpu.VMEM((1, REQ), jnp.int32),
            smem((1, REQ)),
            smem((1, SPAN * CAP)),
            smem((1, SPAN * CAP)),
            smem((1, SLOTS)),
            pltpu.VMEM((REQ, LMAX, HD), BF16),
            pltpu.VMEM((REQ, LMAX, HD), BF16),
            pltpu.VMEM((TP * OUT, QW), BF16),
            pltpu.VMEM((SLOTS * RANK, QW), BF16),
            pltpu.VMEM((SLOTS * RANK, OUT), BF16),
            pltpu.VMEM((REP * RANK_PART, QW), BF16),
            pltpu.VMEM((REP * RANK, OUT_PART), BF16),
            pltpu.VMEM((SPAN, 16, HD), BF16),
            pltpu.VMEM((SPAN, 16, HD), BF16),
            pltpu.VMEM((ROW, 8, 128), jnp.int32),
            pltpu.VMEM((SPAN, 8, HD), F32),
            pltpu.VMEM((32, HD), F32),
            pltpu.VMEM((ROW * REQ, QW), BF16),
            pltpu.VMEM((256, HD), F32),
            pltpu.VMEM((5 * 512, 128), BF16),
            pltpu.VMEM((512, 512), BF16),
            pltpu.VMEM((1, REQ, 128), BF16),
            pltpu.VMEM((REQ, 128), BF16),
            pltpu.VMEM((4, 4, REQ, 128), BF16),
            pltpu.VMEM((ROW * REQ, REP * RANK), BF16),
            pltpu.VMEM((ROW, REQ, OUT_PART), BF16),
            pltpu.VMEM((ROW, REQ, OUT_PART), BF16),
            pltpu.VMEM((4, REQ, OUT), BF16),
            pltpu.VMEM((4, REQ, OUT), BF16),
            pltpu.VMEM((4, REQ, OUT), F32),
            pltpu.VMEM((3, REQ, OUT), BF16),
            pltpu.VMEM((3, REQ, OUT), BF16),
            dma((9,)),
            dma((5,)),
            dma((2,)),
            dma((4, 4)),
            dma((4, 4)),
            dma((4, 4)),
            dma((4, 4)),
            dma((4,)),
            dma((4,)),
            dma((4,)),
            dma((4,)),
            dma((4,)),
            dma((4,)),
            dma((4,)),
            dma((4,)),
            dma((2,)),
            dma((4, 4)),
            dma((4, 4)),
            dma((4,)),
            dma((4,)),
            dma((4,)),
            dma((4,)),
            dma((4,)),
            dma((4,)),
        ],
        compiler_params=pltpu.CompilerParams(
            collective_id=0, has_side_effects=True, vmem_limit_bytes=60 << 20
        ),
    )(
        queries,
        k_cache,
        v_cache,
        new_keys,
        new_values,
        lengths,
        adapter_slot.reshape(1, REQ),
        send_rows,
        recv_rows,
        install,
        out_weight,
        adapter_down.reshape(SLOTS * RANK, QW),
        adapter_up.reshape(SLOTS * RANK, OUT),
        sectioned_down.reshape(RANK, QW),
        sectioned_up.reshape(RANK, OUT),
    )


def solution(mesh):
    placed = (
        P("rep", "tp"),
        P("rep", None, "tp"),
        P("rep", None, "tp"),
        P("rep", "tp"),
        P("rep", "tp"),
        P("rep"),
        P("rep", None),
        P("rep", None),
        P(None, "tp"),
        P("rep", None, "tp"),
        P("rep", None, "tp"),
        P("rep", None, "tp"),
        P("rep", None, "tp"),
        P("rep", None),
        P("rep"),
    )
    return jax.shard_map(
        body, mesh=mesh, in_specs=placed, out_specs=P("rep", "tp"), check_vma=False
    )
```

```python
import functools

import jax
import jax.numpy as jnp
from jax import lax
from jax.experimental import pallas as pl
from jax.experimental.pallas import tpu as pltpu
from jax.sharding import PartitionSpec as P

MESH = pl.DeviceIdType.MESH
F32 = jnp.float32
BF16 = jnp.bfloat16

HD = 128
HEADS = 4
REQ = 32
LMAX = 128
RANK = 64
SLOTS = 8
SPAN = 4
CAP = 2
REP = 32
TP = 8
ROW = 4
QW = HEADS * HD
OUT = 1024
RANK_PART = RANK // ROW
OUT_PART = OUT // ROW
SCALE = HD**-0.5
DISTANCES = (1, 8, 12, 16)
FAR_FIRST = (2, 0, 3, 1)


def iota(shape, dim):
    return lax.broadcasted_iota(jnp.int32, shape, dim)


def dot(a, b):
    return lax.dot_general(a, b, (((1,), (0,)), ((), ())), preferred_element_type=F32)


def dot_nt(a, b):
    return lax.dot_general(a, b, (((1,), (1,)), ((), ())), preferred_element_type=F32)


def remote(src, dst, ssem, rsem, device):
    return pltpu.make_async_remote_copy(
        src_ref=src,
        dst_ref=dst,
        send_sem=ssem,
        recv_sem=rsem,
        device_id=device,
        device_id_type=MESH,
    )


def hops(offset):
    dy, dx = offset // 8, offset % 4
    return min(dy, 4 - dy) + min(dx, 4 - dx) + 4 * ((offset // 4) % 2)


def softmax_parts(scores, own, live):
    scores = jnp.where(live, scores * SCALE, -jnp.inf)
    own = own * SCALE
    top = jnp.maximum(jnp.max(scores, axis=1, keepdims=True), own)
    weights = jnp.exp(scores - top)
    own_weight = jnp.exp(own - top)
    total = jnp.sum(weights, axis=1, keepdims=True) + own_weight
    return weights.astype(BF16), own_weight.astype(BF16).astype(F32), total


def to_column(row, rows):
    spread = jnp.where(iota((rows, 128), 0) == iota((rows, 128), 1), row, 0)
    return jnp.sum(spread.astype(F32), axis=1, keepdims=True).astype(jnp.int32)


def kernel(
    q_hbm,
    k_hbm,
    v_hbm,
    nk_hbm,
    nv_hbm,
    len_hbm,
    slot_hbm,
    send_hbm,
    recv_hbm,
    install_hbm,
    w_hbm,
    adown_hbm,
    aup_hbm,
    sdown_hbm,
    sup_hbm,
    out_ref,
    q_ref,
    nk_ref,
    nv_ref,
    len_row,
    slot_row,
    len_s,
    send_s,
    recv_s,
    install_s,
    kbuf,
    vbuf,
    wbuf,
    adown,
    aup,
    sdn,
    sup,
    qout,
    qin,
    meta,
    res,
    mig,
    merged,
    obuf,
    fold,
    perm,
    msg,
    msg_sib,
    bc,
    sexp,
    dlt_out,
    dlt_in,
    sib_out,
    sib_in,
    rs_own,
    rs_out,
    rs_in,
    sib2_out,
    sib2_in,
    rs2_own,
    rs2_out,
    rs2_in,
    small_sem,
    load_sem,
    s1_local,
    s1_ssem,
    s1_rsem,
    s2_ssem,
    s2_rsem,
    q_ssem,
    q_rsem,
    meta_ssem,
    meta_rsem,
    mig_ssem,
    mig_rsem,
    loc_ssem,
    loc_rsem,
    msg_sem,
    bc_ssem,
    bc_rsem,
    dlt_ssem,
    dlt_rsem,
    sib_ssem,
    sib_rsem,
    rs_ssem,
    rs_rsem,
    sib2_ssem,
    sib2_rsem,
    rs2_ssem,
    rs2_rsem,
):
    r = lax.axis_index("rep")
    t = lax.axis_index("tp")
    x = r % 4
    zh = (r // 4) % 2
    y = r // 8
    row0 = r - x
    z = t // 2
    core = t % 2
    sib = (r, t + 1 - 2 * core)

    other0 = y * 8 + (1 - zh) * 4
    greeted = [((r + o) % REP, t) for o in sorted(range(1, REP), key=hops, reverse=True)]
    greeted += [
        (row0 + (x + xo) % 4, ((z + zo) % 4) * 2 + core)
        for xo in (2, 1, 3, 0)
        for zo in (2, 1, 3)
    ]
    greeted.append(sib)
    barrier = pltpu.get_barrier_semaphore()
    for peer in greeted:
        pl.semaphore_signal(barrier, inc=1, device_id=peer, device_id_type=MESH)

    small = [
        pltpu.make_async_copy(src, dst, small_sem.at[n])
        for n, (src, dst) in enumerate(
            (
                (q_hbm, q_ref),
                (nk_hbm, nk_ref),
                (nv_hbm, nv_ref),
                (recv_hbm, recv_s),
                (install_hbm, install_s),
                (slot_hbm, slot_row),
                (len_hbm, len_row),
                (len_hbm, len_s),
                (send_hbm, send_s),
            )
        )
    ]
    for copy in small:
        copy.start()
    k_load = pltpu.make_async_copy(k_hbm, kbuf, load_sem.at[0])
    v_load = pltpu.make_async_copy(v_hbm, vbuf, load_sem.at[1])
    ad_load = pltpu.make_async_copy(adown_hbm, adown, load_sem.at[2])
    w_load = pltpu.make_async_copy(w_hbm, wbuf, load_sem.at[3])
    au_load = pltpu.make_async_copy(aup_hbm, aup, load_sem.at[4])
    for copy in (k_load, v_load, ad_load, w_load, au_load):
        copy.start()
    for copy in small:
        copy.wait()

    queries = q_ref[...]
    q_heads = jnp.concatenate(
        [queries[:, h * HD : (h + 1) * HD] for h in range(HEADS)], axis=0
    )
    new_keys = nk_ref[...]
    new_values = nv_ref[...]
    stacked = jnp.concatenate([q_heads, new_keys, new_values], axis=0)
    line = iota((64, 192), 0)
    place = line % 16
    col = iota((64, 192), 1)
    kind = jnp.where(
        place < 8,
        place % 4,
        jnp.where(place < 10, 4, jnp.where(place < 12, 5, 9)),
    )
    within = jnp.where(place < 8, place // 4, place % 2)
    entry = (line // 16) * CAP + within
    wanted = jnp.full((64, 192), -1, jnp.int32)
    for j in range(SPAN * CAP):
        wanted = jnp.where(entry == j, recv_s[0, j], wanted)
    pick = (kind == col // REQ) & (wanted == col % REQ)
    gathered = dot(pick.astype(BF16), stacked).astype(BF16)
    for g in range(SPAN):
        qout[g] = gathered[g * 16 : (g + 1) * 16]

    lane1 = iota((1, 128), 1)
    recv4 = jnp.full((1, 128), -1, jnp.int32)
    for j in range(SPAN * CAP):
        recv4 = jnp.where(lane1 // 4 == j, recv_s[0, j], recv4)
    slots = slot_row[...]
    target = jnp.full((1, REQ), -1, jnp.int32)
    for k in range(SLOTS):
        target = jnp.where(slots == k, install_s[0, k], target)
    target = jnp.concatenate([target, jnp.full((1, 128 - REQ), -1, jnp.int32)], axis=1)
    sub8 = iota((8, 128), 0)
    meta[x] = jnp.where(sub8 == 0, recv4, jnp.where(sub8 == 1, target, -1))

    pl.semaphore_wait(barrier, len(greeted))

    sends = []

    q_copies = []
    for g in FAR_FIRST:
        copy = remote(
            qout.at[g],
            qin.at[g],
            q_ssem.at[g],
            q_rsem.at[g],
            ((r + REP - DISTANCES[g]) % REP, t),
        )
        copy.start()
        q_copies.append(copy)
    sends += q_copies

    my_dn = pl.ds(pl.multiple_of(r * RANK_PART, RANK_PART), RANK_PART)
    my_up = pl.ds(pl.multiple_of(r * RANK, RANK), RANK)

    def dn_part(c):
        return sdown_hbm.at[pl.ds(pl.multiple_of(c * RANK_PART, RANK_PART), RANK_PART)]

    def up_part(c):
        return sup_hbm.at[:, pl.ds(pl.multiple_of(c * OUT_PART, OUT_PART), OUT_PART)]

    own_dn = pltpu.make_async_copy(dn_part(x), sdn.at[my_dn], s1_local.at[0])
    own_up = pltpu.make_async_copy(up_part(x), sup.at[my_up], s1_local.at[1])
    own_dn.start()
    own_up.start()
    near_dn, near_up, far_dn, far_up = [], [], [], []
    for o in range(1, 4):
        c = (x + o) % 4
        near_dn.append(
            remote(dn_part(c), sdn.at[my_dn], s1_ssem.at[0, o], s1_rsem.at[0, o], (row0 + c, t))
        )
        near_up.append(
            remote(up_part(c), sup.at[my_up], s1_ssem.at[1, o], s1_rsem.at[1, o], (row0 + c, t))
        )
    for o in range(4):
        c = (x + o) % 4
        far_dn.append(
            remote(dn_part(c), sdn.at[my_dn], s1_ssem.at[2, o], s1_rsem.at[2, o], (other0 + c, t))
        )
        far_up.append(
            remote(up_part(c), sup.at[my_up], s1_ssem.at[3, o], s1_rsem.at[3, o], (other0 + c, t))
        )
    for copy in far_dn + near_dn + near_up:
        copy.start()
    sends += near_dn + near_up + far_dn + far_up

    meta_copies = []
    for o in range(1, 4):
        copy = remote(
            meta.at[x], meta.at[x], meta_ssem.at[o], meta_rsem.at[o], (row0 + (x + o) % 4, t)
        )
        copy.start()
        meta_copies.append(copy)
    sends += meta_copies

    def stage2(half, tag):
        first = y * 8 + half * 4
        dn_rows = pl.ds(pl.multiple_of(first * RANK_PART, 4 * RANK_PART), 4 * RANK_PART)
        up_rows = pl.ds(pl.multiple_of(first * RANK, 4 * RANK), 4 * RANK)
        dn, up = [], []
        for o in range(1, 4):
            peer = ((r + 8 * o) % REP, t)
            dn.append(
                remote(
                    sdn.at[dn_rows], sdn.at[dn_rows], s2_ssem.at[tag, o], s2_rsem.at[tag, o], peer
                )
            )
            up.append(
                remote(
                    sup.at[up_rows],
                    sup.at[up_rows],
                    s2_ssem.at[2 + tag, o],
                    s2_rsem.at[2 + tag, o],
                    peer,
                )
            )
        return dn, up

    s2_near_dn, s2_near_up = stage2(zh, 0)
    s2_far_dn, s2_far_up = stage2(1 - zh, 1)
    sends += s2_near_dn + s2_near_up + s2_far_dn + s2_far_up

    order = (2, 1, 3, 0)

    class Wave:
        def __init__(self, rows, own, sib_out, sib_in, out, arriving, sems):
            self.rows, self.own, self.out, self.arriving = rows, own, out, arriving
            self.sib_out, self.sib_in, self.sems = sib_out, sib_in, sems
            self.sib_copies, self.copies = [], []

        def project(self, zq, cq):
            first = pl.multiple_of((zq * 2 + cq) * OUT, OUT)
            return dot_nt(self.rows, wbuf[pl.ds(first, OUT), :])

        def opposite(self, n):
            self.sib_out[n] = self.fit(self.project((z + order[n]) % 4, 1 - core)).astype(BF16)
            copy = remote(
                self.sib_out.at[n], self.sib_in.at[n], self.sems[0].at[n], self.sems[1].at[n], sib
            )
            copy.start()
            self.sib_copies.append(copy)

        def same(self, n):
            self.own[n] = self.fit(self.project((z + order[n]) % 4, core))

        def pass_on(self, n):
            zq = (z + order[n]) % 4
            self.sib_copies[n].wait_recv()
            both = self.own[n] + self.sib_in[n].astype(F32)
            if order[n] == 0:
                self.own[n] = both
                return
            self.out[n] = both.astype(BF16)
            copy = remote(
                self.out.at[n],
                self.arriving.at[n],
                self.sems[2].at[n],
                self.sems[3].at[n],
                (r, zq * 2 + core),
            )
            copy.start()
            self.copies.append(copy)

        def total(self):
            acc = self.own[3]
            for n, copy in enumerate(self.copies):
                copy.wait_recv()
                acc = acc + self.arriving[n].astype(F32)
            return acc

        def fit(self, block):
            if block.shape[0] == REQ:
                return block
            return jnp.concatenate([block[:8, : OUT // 2], block[:8, OUT // 2 :]], axis=0)

    own_dn.wait()
    for copy in near_dn:
        copy.wait_recv()
    for copy in s2_near_dn:
        copy.start()

    k_load.wait()
    for copy in q_copies:
        copy.wait_recv()
    head8 = iota((8, HD), 0) // HEADS == 0
    line32 = iota((32, 128), 0) // HEADS
    moved_len = jnp.zeros((32, 128), jnp.int32)
    moved_scores, moved_own, moved_values, places = [], [], [], []
    for g in range(SPAN):
        arrived = qin[g]
        arrived_f = arrived.astype(F32)
        q8 = arrived[0:8]
        parts = []
        for i in range(CAP):
            j = g * CAP + i
            at = jnp.maximum(send_s[0, j], 0)
            places.append(at)
            parts.append(dot_nt(q8, kbuf[at]))
            moved_len = jnp.where(line32 == j, len_s[0, at], moved_len)
        moved_scores.append(jnp.where(head8, parts[0], parts[1]))
        key = jnp.where(head8, arrived_f[8:9], arrived_f[9:10])
        moved_own.append(jnp.sum(arrived_f[0:8] * key, axis=1, keepdims=True))
        moved_values.append(jnp.where(head8, arrived_f[10:11], arrived_f[11:12]))
    m_weights, m_own, m_total = softmax_parts(
        jnp.concatenate(moved_scores, axis=0),
        jnp.concatenate(moved_own, axis=0),
        iota((32, 128), 1) < moved_len,
    )
    v_load.wait()
    m_summed = []
    m_wf = m_weights.astype(F32)
    for g in range(SPAN):
        w8 = m_wf[g * 8 : (g + 1) * 8].astype(BF16)
        a = dot(w8, vbuf[places[g * CAP]])
        b = dot(w8, vbuf[places[g * CAP + 1]])
        m_summed.append(jnp.where(head8, a, b))
    m_out = (
        jnp.concatenate(m_summed, axis=0) + m_own * jnp.concatenate(moved_values, axis=0)
    ) / m_total
    m_out = m_out.astype(BF16).astype(F32)
    for g in range(SPAN):
        res[g] = m_out[g * 8 : (g + 1) * 8]

    own_results = []
    for g in FAR_FIRST:
        home = (r + DISTANCES[g]) % REP
        home_x = home % 4
        dst = mig.at[home_x, pl.ds(8 * g, 8)]
        for o in (2, 1, 3, 0):
            device = home - home_x + (home_x + o) % 4
            copy = remote(
                res.at[g], dst, mig_ssem.at[g, o], mig_rsem.at[home_x, g], (device, t)
            )
            if g == 0 and o:
                stays = pltpu.make_async_copy(res.at[g], dst, mig_rsem.at[home_x, g])

                @pl.when(device == r)
                def _():
                    stays.start()

                @pl.when(device != r)
                def _():
                    copy.start()

                own_results.append((copy, device))
            else:
                copy.start()
                sends.append(copy)
    for copy in far_up:
        copy.start()

    er = iota((256, 128), 0)
    ec = iota((256, 128), 1)
    spread_q = ((er % 8 == ec // REQ) & (er // 8 == ec % REQ)).astype(BF16)
    q_local = dot(spread_q, q_heads)
    spread_r = iota((256, REQ), 0) // 8 == iota((256, REQ), 1)
    new_kv = dot(spread_r.astype(BF16), jnp.concatenate([new_keys, new_values], axis=1))
    lengths = jnp.sum(
        jnp.where(spread_r, len_row[...], 0).astype(F32), axis=1, keepdims=True
    ).astype(jnp.int32)
    scores = lax.dot_general(
        q_local.reshape(REQ, 8, HD).astype(BF16),
        kbuf[...],
        (((2,), (2,)), ((0,), (0,))),
        preferred_element_type=F32,
    ).reshape(256, LMAX)
    own = jnp.sum(q_local * new_kv[:, :HD], axis=1, keepdims=True)
    weights, own_b, total = softmax_parts(scores, own, ec < lengths)
    summed = lax.dot_general(
        weights.reshape(REQ, 8, LMAX),
        vbuf[...],
        (((2,), (1,)), ((0,), (0,))),
        preferred_element_type=F32,
    ).reshape(256, HD)
    obuf[...] = (summed + own_b * new_kv[:, HD:]) / total
    here = jnp.concatenate(
        [obuf[pl.ds(h, REQ, stride=8), :] for h in range(HEADS)], axis=1
    ).astype(BF16)

    fc = iota((5 * 512, 128), 0)
    fl = iota((5 * 512, 128), 1)
    block = fc // 512
    goal = jnp.where(block < 4, block * RANK_PART + fc % RANK_PART, 64 + fc % RANK)
    fold[...] = (fl == goal).astype(BF16)
    pc = iota((512, 512), 0)
    pj = iota((512, 512), 1)
    inner = pc % 128
    hit = (
        (inner < 64)
        & (inner // RANK_PART == pj // 128)
        & (pj % 64 == (pc // 128) * RANK_PART + pc % RANK_PART)
    )
    perm[...] = hit.astype(BF16)

    my_rows = pl.ds(pl.multiple_of(x * REQ, REQ), REQ)
    merged[my_rows, :] = here
    row_copies = []
    for o in (2, 1, 3):
        copy = remote(
            merged.at[my_rows],
            merged.at[my_rows],
            loc_ssem.at[o],
            loc_rsem.at[o],
            (row0 + (x + o) % 4, t),
        )
        copy.start()
        row_copies.append(copy)
    sends += row_copies
    stay = Wave(
        here, rs_own, sib_out, sib_in, rs_out, rs_in, (sib_ssem, sib_rsem, rs_ssem, rs_rsem)
    )
    w_load.wait()
    stay.opposite(0)
    stay.same(0)

    for copy in far_dn:
        copy.wait_recv()
    for copy in s2_far_dn:
        copy.start()
    own_up.wait()
    for copy in near_up:
        copy.wait_recv()
    for copy in s2_near_up:
        copy.start()

    stay.opposite(1)
    stay.pass_on(0)
    stay.same(1)
    stay.opposite(2)
    stay.pass_on(1)
    stay.same(2)
    stay.opposite(3)
    stay.pass_on(2)
    stay.same(3)
    stay.pass_on(3)

    def arrived_at(h):
        for g in range(SPAN):
            remote(
                res.at[0], mig.at[h, pl.ds(8 * g, 8)], mig_ssem.at[g, 0], mig_rsem.at[h, g], sib
            ).wait_recv()

    mh = iota((128, 32), 0)
    ml = iota((128, 32), 1)

    def put_rows(recv_row, results, rows):
        put = ((mh % REQ == recv_row) & (mh // REQ == ml % 4)).astype(BF16)
        placed = dot(put, results.astype(BF16)).astype(BF16)
        placed = jnp.concatenate([placed[k * REQ : (k + 1) * REQ] for k in range(HEADS)], axis=1)
        hit = jnp.where(iota((REQ, 32), 0) == recv_row, 1.0, 0.0)
        taken = jnp.max(hit, axis=1, keepdims=True) > 0.5
        return jnp.where(taken, placed, rows), taken

    arrived_at(x)
    mine, taken = put_rows(recv4[:, 0:32], mig[x], here)
    moved = jnp.concatenate([mig[x, pl.ds(h, 8, stride=HEADS), :] for h in range(HEADS)], axis=1)
    moved = jnp.concatenate([moved, jnp.zeros_like(moved)], axis=0).astype(BF16)
    move = Wave(
        moved,
        rs2_own,
        sib2_out,
        sib2_in,
        rs2_out,
        rs2_in,
        (sib2_ssem, sib2_rsem, rs2_ssem, rs2_rsem),
    )
    move.opposite(0)
    move.same(0)
    move.opposite(1)
    move.pass_on(0)

    ad_load.wait()
    slot_col = to_column(
        jnp.concatenate([slots, jnp.full((1, 128 - REQ), -1, jnp.int32)], axis=1), REQ
    )
    resident = to_column(target, REQ) < 0
    c512 = iota((REQ, 512), 1)
    part = dot_nt(mine, adown[...])
    pieces = [jnp.where((c512 // RANK == slot_col) & resident, part, 0.0)]
    for copy in meta_copies + row_copies:
        copy.wait_recv()
    for o in range(1, 4):
        arrived_at((x + o) % 4)
    tiles = [meta[h] for h in range(ROW)]
    tcols = [to_column(tile[1:2], REQ) for tile in tiles]
    together = jnp.concatenate(
        [
            put_rows(tiles[h][0:1, 0:32], mig[h], merged[h * REQ : (h + 1) * REQ, :])[0]
            for h in range(ROW)
        ],
        axis=0,
    )
    for copy in s2_near_dn + s2_far_dn:
        copy.wait_recv()
    part = dot_nt(together, sdn[...])
    sections = [
        jnp.where(c512 // RANK_PART == tcols[h], part[h * REQ : (h + 1) * REQ], 0.0)
        for h in range(ROW)
    ]
    masked = jnp.concatenate(sections + pieces, axis=1).astype(BF16)
    msg[0] = dot(masked, fold[...]).astype(BF16)
    msg_copy = remote(msg.at[0], msg_sib, msg_sem.at[0], msg_sem.at[1], sib)
    msg_copy.start()
    for copy in far_up:
        copy.wait_recv()
    for copy in s2_far_up:
        copy.start()
    move.same(1)
    move.opposite(2)
    move.pass_on(1)
    msg_copy.wait_recv()
    bc[x, z] = (msg[0].astype(F32) + msg_sib[...].astype(F32)).astype(BF16)
    bc_copies = []
    for xo in range(4):
        for zo in range(4):
            if xo == 0 and zo == 0:
                continue
            copy = remote(
                bc.at[x, z],
                bc.at[x, z],
                bc_ssem.at[xo, zo],
                bc_rsem.at[xo, zo],
                (row0 + (x + xo) % 4, ((z + zo) % 4) * 2 + core),
            )
            copy.start()
            bc_copies.append(copy)
    sends += bc_copies
    move.same(2)
    move.opposite(3)
    move.pass_on(2)
    move.same(3)
    move.pass_on(3)

    for copy in bc_copies:
        copy.wait_recv()
    sums = []
    for h in range(ROW):
        sums.append(
            (bc[h, 0].astype(F32) + bc[h, 1].astype(F32))
            + (bc[h, 2].astype(F32) + bc[h, 3].astype(F32))
        )
    shrunk = dot(jnp.concatenate(sums, axis=1).astype(BF16), perm[...])
    lane = iota((REQ, 128), 1)
    for h in range(ROW):
        ranks = shrunk[:, h * 128 : (h + 1) * 128]
        for n in range(16):
            sexp[h * REQ : (h + 1) * REQ, n * 128 : (n + 1) * 128] = jnp.where(
                lane // RANK + 2 * n == tcols[h], ranks, 0.0
            ).astype(BF16)
    for copy in s2_near_up + s2_far_up:
        copy.wait_recv()
    delta = dot(sexp[...], sup[...])
    dlt_copies = []
    for h in range(ROW):
        dlt_out[h] = delta[h * REQ : (h + 1) * REQ].astype(BF16)
    dlt_in[x] = dlt_out[x]
    for o in range(1, 4):
        c = (x + o) % 4
        copy = remote(
            dlt_out.at[c], dlt_in.at[x], dlt_ssem.at[o], dlt_rsem.at[o], (row0 + c, t)
        )
        copy.start()
        dlt_copies.append(copy)
    sends += dlt_copies

    au_load.wait()
    own_sum = (bc[x, 0].astype(F32) + bc[x, 1].astype(F32)) + (
        bc[x, 2].astype(F32) + bc[x, 3].astype(F32)
    )
    ranks = jnp.where(lane < RANK, pltpu.roll(own_sum, RANK, 1), own_sum)
    spread = jnp.concatenate(
        [
            jnp.where((lane // RANK + 2 * n == slot_col) & resident, ranks, 0.0)
            for n in range(SLOTS // 2)
        ],
        axis=1,
    ).astype(BF16)
    acc = dot(spread, aup[...])

    folded = move.total()
    moved_sum = jnp.concatenate([folded[:8], folded[8:]], axis=1)
    high = moved_sum.astype(BF16)
    low = (moved_sum - high.astype(F32)).astype(BF16)
    both = jnp.concatenate([high, low], axis=0)
    l16 = iota((REQ, 16), 1) % 8
    into = jnp.full((REQ, 16), -1, jnp.int32)
    for j in range(SPAN * CAP):
        into = jnp.where(l16 == j, recv_s[0, j], into)
    replaced = dot((into == iota((REQ, 16), 0)).astype(BF16), both)
    acc = acc + jnp.where(taken, replaced, stay.total())
    for copy in dlt_copies:
        copy.wait_recv()
    out_ref[...] = (
        acc + jnp.concatenate([dlt_in[h].astype(F32) for h in range(ROW)], axis=1)
    ).astype(BF16)

    msg_copy.wait_send()
    for copy in stay.sib_copies + stay.copies + move.sib_copies + move.copies + sends:
        copy.wait_send()
    for copy, device in own_results:

        @pl.when(device != r)
        def _():
            copy.wait_send()


def body(
    queries,
    k_cache,
    v_cache,
    new_keys,
    new_values,
    kv_len,
    send_rows,
    recv_rows,
    out_weight,
    adapter_down,
    adapter_up,
    sectioned_down,
    sectioned_up,
    install,
    adapter_slot,
):
    vmem = pl.BlockSpec(memory_space=pltpu.VMEM)
    hbm = pl.BlockSpec(memory_space=pltpu.HBM)
    smem = functools.partial(pltpu.SMEM, dtype=jnp.int32)
    dma = pltpu.SemaphoreType.DMA
    lengths = kv_len.reshape(1, REQ)
    return pl.pallas_call(
        kernel,
        out_shape=jax.ShapeDtypeStruct((REQ, OUT), BF16),
        in_specs=[hbm] * 15,
        out_specs=vmem,
        scratch_shapes=[
            pltpu.VMEM((REQ, QW), BF16),
            pltpu.VMEM((REQ, HD), BF16),
            pltpu.VMEM((REQ, HD), BF16),
            pltpu.VMEM((1, REQ), jnp.int32),
            pltpu.VMEM((1, REQ), jnp.int32),
            smem((1, REQ)),
            smem((1, SPAN * CAP)),
            smem((1, SPAN * CAP)),
            smem((1, SLOTS)),
            pltpu.VMEM((REQ, LMAX, HD), BF16),
            pltpu.VMEM((REQ, LMAX, HD), BF16),
            pltpu.VMEM((TP * OUT, QW), BF16),
            pltpu.VMEM((SLOTS * RANK, QW), BF16),
            pltpu.VMEM((SLOTS * RANK, OUT), BF16),
            pltpu.VMEM((REP * RANK_PART, QW), BF16),
            pltpu.VMEM((REP * RANK, OUT_PART), BF16),
            pltpu.VMEM((SPAN, 16, HD), BF16),
            pltpu.VMEM((SPAN, 16, HD), BF16),
            pltpu.VMEM((ROW, 8, 128), jnp.int32),
            pltpu.VMEM((SPAN, 8, HD), F32),
            pltpu.VMEM((ROW, 32, HD), F32),
            pltpu.VMEM((ROW * REQ, QW), BF16),
            pltpu.VMEM((256, HD), F32),
            pltpu.VMEM((5 * 512, 128), BF16),
            pltpu.VMEM((512, 512), BF16),
            pltpu.VMEM((1, REQ, 128), BF16),
            pltpu.VMEM((REQ, 128), BF16),
            pltpu.VMEM((4, 4, REQ, 128), BF16),
            pltpu.VMEM((ROW * REQ, REP * RANK), BF16),
            pltpu.VMEM((ROW, REQ, OUT_PART), BF16),
            pltpu.VMEM((ROW, REQ, OUT_PART), BF16),
            pltpu.VMEM((4, REQ, OUT), BF16),
            pltpu.VMEM((4, REQ, OUT), BF16),
            pltpu.VMEM((4, REQ, OUT), F32),
            pltpu.VMEM((3, REQ, OUT), BF16),
            pltpu.VMEM((3, REQ, OUT), BF16),
            pltpu.VMEM((4, 16, OUT // 2), BF16),
            pltpu.VMEM((4, 16, OUT // 2), BF16),
            pltpu.VMEM((4, 16, OUT // 2), F32),
            pltpu.VMEM((3, 16, OUT // 2), BF16),
            pltpu.VMEM((3, 16, OUT // 2), BF16),
            dma((9,)),
            dma((5,)),
            dma((2,)),
            dma((4, 4)),
            dma((4, 4)),
            dma((4, 4)),
            dma((4, 4)),
            dma((4,)),
            dma((4,)),
            dma((4,)),
            dma((4,)),
            dma((4, 4)),
            dma((4, 4)),
            dma((4,)),
            dma((4,)),
            dma((2,)),
            dma((4, 4)),
            dma((4, 4)),
            dma((4,)),
            dma((4,)),
            dma((4,)),
            dma((4,)),
            dma((4,)),
            dma((4,)),
            dma((4,)),
            dma((4,)),
            dma((4,)),
            dma((4,)),
        ],
        compiler_params=pltpu.CompilerParams(
            collective_id=0, has_side_effects=True, vmem_limit_bytes=60 << 20
        ),
    )(
        queries,
        k_cache,
        v_cache,
        new_keys,
        new_values,
        lengths,
        adapter_slot.reshape(1, REQ),
        send_rows,
        recv_rows,
        install,
        out_weight,
        adapter_down.reshape(SLOTS * RANK, QW),
        adapter_up.reshape(SLOTS * RANK, OUT),
        sectioned_down.reshape(RANK, QW),
        sectioned_up.reshape(RANK, OUT),
    )


def solution(mesh):
    placed = (
        P("rep", "tp"),
        P("rep", None, "tp"),
        P("rep", None, "tp"),
        P("rep", "tp"),
        P("rep", "tp"),
        P("rep"),
        P("rep", None),
        P("rep", None),
        P(None, "tp"),
        P("rep", None, "tp"),
        P("rep", None, "tp"),
        P("rep", None, "tp"),
        P("rep", None, "tp"),
        P("rep", None),
        P("rep"),
    )
    return jax.shard_map(
        body, mesh=mesh, in_specs=placed, out_specs=P("rep", "tp"), check_vma=False
    )
```

```python
import functools

import jax
import jax.numpy as jnp
from jax import lax
from jax.experimental import pallas as pl
from jax.experimental.pallas import tpu as pltpu
from jax.sharding import PartitionSpec as P

MESH = pl.DeviceIdType.MESH
F32 = jnp.float32
BF16 = jnp.bfloat16

HD = 128
HEADS = 4
REQ = 32
LMAX = 128
RANK = 64
SLOTS = 8
SPAN = 4
CAP = 2
REP = 32
TP = 8
ROW = 4
QW = HEADS * HD
OUT = 1024
RANK_PART = RANK // ROW
OUT_PART = OUT // ROW
SCALE = HD**-0.5
DISTANCES = (1, 8, 12, 16)
FAR_FIRST = (2, 0, 3, 1)


def iota(shape, dim):
    return lax.broadcasted_iota(jnp.int32, shape, dim)


def dot(a, b):
    return lax.dot_general(a, b, (((1,), (0,)), ((), ())), preferred_element_type=F32)


def dot_nt(a, b):
    return lax.dot_general(a, b, (((1,), (1,)), ((), ())), preferred_element_type=F32)


def remote(src, dst, ssem, rsem, device):
    return pltpu.make_async_remote_copy(
        src_ref=src,
        dst_ref=dst,
        send_sem=ssem,
        recv_sem=rsem,
        device_id=device,
        device_id_type=MESH,
    )


def hops(offset):
    dy, dx = offset // 8, offset % 4
    return min(dy, 4 - dy) + min(dx, 4 - dx) + 4 * ((offset // 4) % 2)


def softmax_parts(scores, own, live):
    scores = jnp.where(live, scores * SCALE, -jnp.inf)
    own = own * SCALE
    top = jnp.maximum(jnp.max(scores, axis=1, keepdims=True), own)
    weights = jnp.exp(scores - top)
    own_weight = jnp.exp(own - top)
    total = jnp.sum(weights, axis=1, keepdims=True) + own_weight
    return weights.astype(BF16), own_weight.astype(BF16).astype(F32), total


def to_column(row, rows):
    spread = jnp.where(iota((rows, 128), 0) == iota((rows, 128), 1), row, 0)
    return jnp.sum(spread.astype(F32), axis=1, keepdims=True).astype(jnp.int32)


def kernel(
    q_hbm,
    k_hbm,
    v_hbm,
    nk_hbm,
    nv_hbm,
    len_hbm,
    slot_hbm,
    send_hbm,
    recv_hbm,
    install_hbm,
    w_hbm,
    adown_hbm,
    aup_hbm,
    sdown_hbm,
    sup_hbm,
    out_ref,
    q_ref,
    nk_ref,
    nv_ref,
    len_row,
    slot_row,
    len_s,
    send_s,
    recv_s,
    install_s,
    kbuf,
    vbuf,
    wbuf,
    adown,
    aup,
    sdn,
    sup,
    qout,
    qin,
    meta,
    res,
    mig,
    merged,
    obuf,
    fold,
    perm,
    msg,
    msg_sib,
    bc,
    sexp,
    dlt_out,
    dlt_in,
    sib_out,
    sib_in,
    rs_own,
    rs_out,
    rs_in,
    sib2_out,
    sib2_in,
    rs2_own,
    rs2_out,
    rs2_in,
    small_sem,
    load_sem,
    s1_local,
    s1_ssem,
    s1_rsem,
    s2_ssem,
    s2_rsem,
    q_ssem,
    q_rsem,
    meta_ssem,
    meta_rsem,
    mig_ssem,
    mig_rsem,
    loc_ssem,
    loc_rsem,
    msg_sem,
    bc_ssem,
    bc_rsem,
    dlt_ssem,
    dlt_rsem,
    sib_ssem,
    sib_rsem,
    rs_ssem,
    rs_rsem,
    sib2_ssem,
    sib2_rsem,
    rs2_ssem,
    rs2_rsem,
):
    r = lax.axis_index("rep")
    t = lax.axis_index("tp")
    x = r % 4
    zh = (r // 4) % 2
    y = r // 8
    row0 = r - x
    z = t // 2
    core = t % 2
    sib = (r, t + 1 - 2 * core)

    other0 = y * 8 + (1 - zh) * 4
    greeted = [((r + o) % REP, t) for o in sorted(range(1, REP), key=hops, reverse=True)]
    greeted += [
        (row0 + (x + xo) % 4, ((z + zo) % 4) * 2 + core)
        for xo in (2, 1, 3, 0)
        for zo in (2, 1, 3)
    ]
    greeted.append(sib)
    barrier = pltpu.get_barrier_semaphore()
    for peer in greeted:
        pl.semaphore_signal(barrier, inc=1, device_id=peer, device_id_type=MESH)

    small = [
        pltpu.make_async_copy(src, dst, small_sem.at[n])
        for n, (src, dst) in enumerate(
            (
                (q_hbm, q_ref),
                (nk_hbm, nk_ref),
                (nv_hbm, nv_ref),
                (recv_hbm, recv_s),
                (install_hbm, install_s),
                (slot_hbm, slot_row),
                (len_hbm, len_row),
                (len_hbm, len_s),
                (send_hbm, send_s),
            )
        )
    ]
    for copy in small:
        copy.start()
    k_load = pltpu.make_async_copy(k_hbm, kbuf, load_sem.at[0])
    v_load = pltpu.make_async_copy(v_hbm, vbuf, load_sem.at[1])
    ad_load = pltpu.make_async_copy(adown_hbm, adown, load_sem.at[2])
    w_load = pltpu.make_async_copy(w_hbm, wbuf, load_sem.at[3])
    au_load = pltpu.make_async_copy(aup_hbm, aup, load_sem.at[4])
    for copy in (k_load, v_load, ad_load, w_load, au_load):
        copy.start()
    for copy in small:
        copy.wait()

    queries = q_ref[...]
    q_heads = jnp.concatenate(
        [queries[:, h * HD : (h + 1) * HD] for h in range(HEADS)], axis=0
    )
    new_keys = nk_ref[...]
    new_values = nv_ref[...]
    stacked = jnp.concatenate([q_heads, new_keys, new_values], axis=0)
    line = iota((64, 192), 0)
    place = line % 16
    col = iota((64, 192), 1)
    kind = jnp.where(
        place < 8,
        place % 4,
        jnp.where(place < 10, 4, jnp.where(place < 12, 5, 9)),
    )
    within = jnp.where(place < 8, place // 4, place % 2)
    entry = (line // 16) * CAP + within
    wanted = jnp.full((64, 192), -1, jnp.int32)
    for j in range(SPAN * CAP):
        wanted = jnp.where(entry == j, recv_s[0, j], wanted)
    pick = (kind == col // REQ) & (wanted == col % REQ)
    gathered = dot(pick.astype(BF16), stacked).astype(BF16)
    for g in range(SPAN):
        qout[g] = gathered[g * 16 : (g + 1) * 16]

    lane1 = iota((1, 128), 1)
    recv4 = jnp.full((1, 128), -1, jnp.int32)
    for j in range(SPAN * CAP):
        recv4 = jnp.where(lane1 // 4 == j, recv_s[0, j], recv4)
    slots = slot_row[...]
    target = jnp.full((1, REQ), -1, jnp.int32)
    for k in range(SLOTS):
        target = jnp.where(slots == k, install_s[0, k], target)
    target = jnp.concatenate([target, jnp.full((1, 128 - REQ), -1, jnp.int32)], axis=1)
    sub8 = iota((8, 128), 0)
    meta[x] = jnp.where(sub8 == 0, recv4, jnp.where(sub8 == 1, target, -1))

    pl.semaphore_wait(barrier, len(greeted))

    sends = []

    q_copies = []
    for g in FAR_FIRST:
        copy = remote(
            qout.at[g],
            qin.at[g],
            q_ssem.at[g],
            q_rsem.at[g],
            ((r + REP - DISTANCES[g]) % REP, t),
        )
        copy.start()
        q_copies.append(copy)
    sends += q_copies

    my_dn = pl.ds(pl.multiple_of(r * RANK_PART, RANK_PART), RANK_PART)
    my_up = pl.ds(pl.multiple_of(r * RANK, RANK), RANK)

    def dn_part(c):
        return sdown_hbm.at[pl.ds(pl.multiple_of(c * RANK_PART, RANK_PART), RANK_PART)]

    def up_part(c):
        return sup_hbm.at[:, pl.ds(pl.multiple_of(c * OUT_PART, OUT_PART), OUT_PART)]

    own_dn = pltpu.make_async_copy(dn_part(x), sdn.at[my_dn], s1_local.at[0])
    own_up = pltpu.make_async_copy(up_part(x), sup.at[my_up], s1_local.at[1])
    own_dn.start()
    own_up.start()
    near_dn, near_up, far_dn, far_up = [], [], [], []
    for o in range(1, 4):
        c = (x + o) % 4
        near_dn.append(
            remote(dn_part(c), sdn.at[my_dn], s1_ssem.at[0, o], s1_rsem.at[0, o], (row0 + c, t))
        )
        near_up.append(
            remote(up_part(c), sup.at[my_up], s1_ssem.at[1, o], s1_rsem.at[1, o], (row0 + c, t))
        )
    for o in range(4):
        c = (x + o) % 4
        far_dn.append(
            remote(dn_part(c), sdn.at[my_dn], s1_ssem.at[2, o], s1_rsem.at[2, o], (other0 + c, t))
        )
        far_up.append(
            remote(up_part(c), sup.at[my_up], s1_ssem.at[3, o], s1_rsem.at[3, o], (other0 + c, t))
        )
    for copy in far_dn + near_dn + near_up:
        copy.start()
    sends += near_dn + near_up + far_dn + far_up

    meta_copies = []
    for o in range(1, 4):
        copy = remote(
            meta.at[x], meta.at[x], meta_ssem.at[o], meta_rsem.at[o], (row0 + (x + o) % 4, t)
        )
        copy.start()
        meta_copies.append(copy)
    sends += meta_copies

    def stage2(half, tag):
        first = y * 8 + half * 4
        dn_rows = pl.ds(pl.multiple_of(first * RANK_PART, 4 * RANK_PART), 4 * RANK_PART)
        up_rows = pl.ds(pl.multiple_of(first * RANK, 4 * RANK), 4 * RANK)
        dn, up = [], []
        for o in range(1, 4):
            peer = ((r + 8 * o) % REP, t)
            dn.append(
                remote(
                    sdn.at[dn_rows], sdn.at[dn_rows], s2_ssem.at[tag, o], s2_rsem.at[tag, o], peer
                )
            )
            up.append(
                remote(
                    sup.at[up_rows],
                    sup.at[up_rows],
                    s2_ssem.at[2 + tag, o],
                    s2_rsem.at[2 + tag, o],
                    peer,
                )
            )
        return dn, up

    s2_near_dn, s2_near_up = stage2(zh, 0)
    s2_far_dn, s2_far_up = stage2(1 - zh, 1)
    sends += s2_near_dn + s2_near_up + s2_far_dn + s2_far_up

    order = (2, 1, 3, 0)

    class Wave:
        def __init__(self, rows, own, sib_out, sib_in, out, arriving, sems):
            self.rows, self.own, self.out, self.arriving = rows, own, out, arriving
            self.sib_out, self.sib_in, self.sems = sib_out, sib_in, sems
            self.sib_copies, self.copies = [], []

        def project(self, zq, cq):
            first = pl.multiple_of((zq * 2 + cq) * OUT, OUT)
            return dot_nt(self.rows, wbuf[pl.ds(first, OUT), :])

        def opposite(self, n):
            self.sib_out[n] = self.fit(self.project((z + order[n]) % 4, 1 - core)).astype(BF16)
            copy = remote(
                self.sib_out.at[n], self.sib_in.at[n], self.sems[0].at[n], self.sems[1].at[n], sib
            )
            copy.start()
            self.sib_copies.append(copy)

        def same(self, n):
            self.own[n] = self.fit(self.project((z + order[n]) % 4, core))

        def pass_on(self, n):
            zq = (z + order[n]) % 4
            self.sib_copies[n].wait_recv()
            both = self.own[n] + self.sib_in[n].astype(F32)
            if order[n] == 0:
                self.own[n] = both
                return
            self.out[n] = both.astype(BF16)
            copy = remote(
                self.out.at[n],
                self.arriving.at[n],
                self.sems[2].at[n],
                self.sems[3].at[n],
                (r, zq * 2 + core),
            )
            copy.start()
            self.copies.append(copy)

        def total(self):
            acc = self.own[3]
            for n, copy in enumerate(self.copies):
                copy.wait_recv()
                acc = acc + self.arriving[n].astype(F32)
            return acc

        def fit(self, block):
            if block.shape[0] == REQ:
                return block
            return jnp.concatenate([block[:8, : OUT // 2], block[:8, OUT // 2 :]], axis=0)

    own_dn.wait()
    for copy in near_dn:
        copy.wait_recv()
    for copy in s2_near_dn:
        copy.start()

    k_load.wait()
    for copy in far_up:
        copy.start()
    for copy in q_copies:
        copy.wait_recv()
    head8 = iota((8, HD), 0) // HEADS == 0
    line32 = iota((32, 128), 0) // HEADS
    moved_len = jnp.zeros((32, 128), jnp.int32)
    moved_scores, moved_own, moved_values, places = [], [], [], []
    for g in range(SPAN):
        arrived = qin[g]
        arrived_f = arrived.astype(F32)
        q8 = arrived[0:8]
        parts = []
        for i in range(CAP):
            j = g * CAP + i
            at = jnp.maximum(send_s[0, j], 0)
            places.append(at)
            parts.append(dot_nt(q8, kbuf[at]))
            moved_len = jnp.where(line32 == j, len_s[0, at], moved_len)
        moved_scores.append(jnp.where(head8, parts[0], parts[1]))
        key = jnp.where(head8, arrived_f[8:9], arrived_f[9:10])
        moved_own.append(jnp.sum(arrived_f[0:8] * key, axis=1, keepdims=True))
        moved_values.append(jnp.where(head8, arrived_f[10:11], arrived_f[11:12]))
    m_weights, m_own, m_total = softmax_parts(
        jnp.concatenate(moved_scores, axis=0),
        jnp.concatenate(moved_own, axis=0),
        iota((32, 128), 1) < moved_len,
    )
    v_load.wait()
    m_summed = []
    m_wf = m_weights.astype(F32)
    for g in range(SPAN):
        w8 = m_wf[g * 8 : (g + 1) * 8].astype(BF16)
        a = dot(w8, vbuf[places[g * CAP]])
        b = dot(w8, vbuf[places[g * CAP + 1]])
        m_summed.append(jnp.where(head8, a, b))
    m_out = (
        jnp.concatenate(m_summed, axis=0) + m_own * jnp.concatenate(moved_values, axis=0)
    ) / m_total
    m_out = m_out.astype(BF16).astype(F32)
    for g in range(SPAN):
        res[g] = m_out[g * 8 : (g + 1) * 8]

    own_results = []
    for g in FAR_FIRST:
        home = (r + DISTANCES[g]) % REP
        home_x = home % 4
        dst = mig.at[home_x, pl.ds(8 * g, 8)]
        for o in (2, 1, 3, 0):
            device = home - home_x + (home_x + o) % 4
            copy = remote(
                res.at[g], dst, mig_ssem.at[g, o], mig_rsem.at[home_x, g], (device, t)
            )
            if g == 0 and o:
                stays = pltpu.make_async_copy(res.at[g], dst, mig_rsem.at[home_x, g])

                @pl.when(device == r)
                def _():
                    stays.start()

                @pl.when(device != r)
                def _():
                    copy.start()

                own_results.append((copy, device))
            else:
                copy.start()
                sends.append(copy)

    er = iota((256, 128), 0)
    ec = iota((256, 128), 1)
    spread_q = ((er % 8 == ec // REQ) & (er // 8 == ec % REQ)).astype(BF16)
    q_local = dot(spread_q, q_heads)
    spread_r = iota((256, REQ), 0) // 8 == iota((256, REQ), 1)
    new_kv = dot(spread_r.astype(BF16), jnp.concatenate([new_keys, new_values], axis=1))
    lengths = jnp.sum(
        jnp.where(spread_r, len_row[...], 0).astype(F32), axis=1, keepdims=True
    ).astype(jnp.int32)
    scores = lax.dot_general(
        q_local.reshape(REQ, 8, HD).astype(BF16),
        kbuf[...],
        (((2,), (2,)), ((0,), (0,))),
        preferred_element_type=F32,
    ).reshape(256, LMAX)
    own = jnp.sum(q_local * new_kv[:, :HD], axis=1, keepdims=True)
    weights, own_b, total = softmax_parts(scores, own, ec < lengths)
    summed = lax.dot_general(
        weights.reshape(REQ, 8, LMAX),
        vbuf[...],
        (((2,), (1,)), ((0,), (0,))),
        preferred_element_type=F32,
    ).reshape(256, HD)
    obuf[...] = (summed + own_b * new_kv[:, HD:]) / total
    here = jnp.concatenate(
        [obuf[pl.ds(h, REQ, stride=8), :] for h in range(HEADS)], axis=1
    ).astype(BF16)

    fc = iota((5 * 512, 128), 0)
    fl = iota((5 * 512, 128), 1)
    block = fc // 512
    goal = jnp.where(block < 4, block * RANK_PART + fc % RANK_PART, 64 + fc % RANK)
    fold[...] = (fl == goal).astype(BF16)
    pc = iota((512, 512), 0)
    pj = iota((512, 512), 1)
    inner = pc % 128
    hit = (
        (inner < 64)
        & (inner // RANK_PART == pj // 128)
        & (pj % 64 == (pc // 128) * RANK_PART + pc % RANK_PART)
    )
    perm[...] = hit.astype(BF16)

    my_rows = pl.ds(pl.multiple_of(x * REQ, REQ), REQ)
    merged[my_rows, :] = here
    row_copies = []
    for o in (2, 1, 3):
        copy = remote(
            merged.at[my_rows],
            merged.at[my_rows],
            loc_ssem.at[o],
            loc_rsem.at[o],
            (row0 + (x + o) % 4, t),
        )
        copy.start()
        row_copies.append(copy)
    sends += row_copies
    stay = Wave(
        here, rs_own, sib_out, sib_in, rs_out, rs_in, (sib_ssem, sib_rsem, rs_ssem, rs_rsem)
    )
    w_load.wait()
    stay.opposite(0)
    stay.same(0)

    for copy in far_dn:
        copy.wait_recv()
    for copy in s2_far_dn:
        copy.start()
    own_up.wait()
    for copy in near_up:
        copy.wait_recv()
    for copy in s2_near_up:
        copy.start()

    stay.opposite(1)
    stay.pass_on(0)
    stay.same(1)
    stay.opposite(2)
    stay.pass_on(1)
    stay.same(2)
    stay.opposite(3)
    stay.pass_on(2)
    stay.same(3)
    stay.pass_on(3)

    def arrived_at(h):
        for g in range(SPAN):
            remote(
                res.at[0], mig.at[h, pl.ds(8 * g, 8)], mig_ssem.at[g, 0], mig_rsem.at[h, g], sib
            ).wait_recv()

    mh = iota((128, 32), 0)
    ml = iota((128, 32), 1)

    def put_rows(recv_row, results, rows):
        put = ((mh % REQ == recv_row) & (mh // REQ == ml % 4)).astype(BF16)
        placed = dot(put, results.astype(BF16)).astype(BF16)
        placed = jnp.concatenate([placed[k * REQ : (k + 1) * REQ] for k in range(HEADS)], axis=1)
        hit = jnp.where(iota((REQ, 32), 0) == recv_row, 1.0, 0.0)
        taken = jnp.max(hit, axis=1, keepdims=True) > 0.5
        return jnp.where(taken, placed, rows), taken

    arrived_at(x)
    mine, taken = put_rows(recv4[:, 0:32], mig[x], here)
    moved = jnp.concatenate([mig[x, pl.ds(h, 8, stride=HEADS), :] for h in range(HEADS)], axis=1)
    moved = jnp.concatenate([moved, jnp.zeros_like(moved)], axis=0).astype(BF16)
    move = Wave(
        moved,
        rs2_own,
        sib2_out,
        sib2_in,
        rs2_out,
        rs2_in,
        (sib2_ssem, sib2_rsem, rs2_ssem, rs2_rsem),
    )

    ad_load.wait()
    slot_col = to_column(
        jnp.concatenate([slots, jnp.full((1, 128 - REQ), -1, jnp.int32)], axis=1), REQ
    )
    resident = to_column(target, REQ) < 0
    c512 = iota((REQ, 512), 1)
    part = dot_nt(mine, adown[...])
    pieces = [jnp.where((c512 // RANK == slot_col) & resident, part, 0.0)]
    for copy in meta_copies + row_copies:
        copy.wait_recv()
    for o in range(1, 4):
        arrived_at((x + o) % 4)
    tiles = [meta[h] for h in range(ROW)]
    tcols = [to_column(tile[1:2], REQ) for tile in tiles]
    together = jnp.concatenate(
        [
            put_rows(tiles[h][0:1, 0:32], mig[h], merged[h * REQ : (h + 1) * REQ, :])[0]
            for h in range(ROW)
        ],
        axis=0,
    )
    for copy in s2_near_dn + s2_far_dn:
        copy.wait_recv()
    part = dot_nt(together, sdn[...])
    sections = [
        jnp.where(c512 // RANK_PART == tcols[h], part[h * REQ : (h + 1) * REQ], 0.0)
        for h in range(ROW)
    ]
    masked = jnp.concatenate(sections + pieces, axis=1).astype(BF16)
    msg[0] = dot(masked, fold[...]).astype(BF16)
    msg_copy = remote(msg.at[0], msg_sib, msg_sem.at[0], msg_sem.at[1], sib)
    msg_copy.start()
    for copy in far_up:
        copy.wait_recv()
    for copy in s2_far_up:
        copy.start()
    move.opposite(0)
    move.same(0)
    msg_copy.wait_recv()
    bc[x, z] = (msg[0].astype(F32) + msg_sib[...].astype(F32)).astype(BF16)
    bc_copies = []
    for xo in range(4):
        for zo in range(4):
            if xo == 0 and zo == 0:
                continue
            copy = remote(
                bc.at[x, z],
                bc.at[x, z],
                bc_ssem.at[xo, zo],
                bc_rsem.at[xo, zo],
                (row0 + (x + xo) % 4, ((z + zo) % 4) * 2 + core),
            )
            copy.start()
            bc_copies.append(copy)
    sends += bc_copies
    move.pass_on(0)
    for n in range(1, 4):
        move.opposite(n)
        move.same(n)
        move.pass_on(n)

    for copy in bc_copies:
        copy.wait_recv()
    sums = []
    for h in range(ROW):
        sums.append(
            (bc[h, 0].astype(F32) + bc[h, 1].astype(F32))
            + (bc[h, 2].astype(F32) + bc[h, 3].astype(F32))
        )
    shrunk = dot(jnp.concatenate(sums, axis=1).astype(BF16), perm[...])
    lane = iota((REQ, 128), 1)
    for h in range(ROW):
        ranks = shrunk[:, h * 128 : (h + 1) * 128]
        for n in range(16):
            sexp[h * REQ : (h + 1) * REQ, n * 128 : (n + 1) * 128] = jnp.where(
                lane // RANK + 2 * n == tcols[h], ranks, 0.0
            ).astype(BF16)
    for copy in s2_near_up + s2_far_up:
        copy.wait_recv()
    delta = dot(sexp[...], sup[...])
    dlt_copies = []
    for h in range(ROW):
        dlt_out[h] = delta[h * REQ : (h + 1) * REQ].astype(BF16)
    dlt_in[x] = dlt_out[x]
    for o in range(1, 4):
        c = (x + o) % 4
        copy = remote(
            dlt_out.at[c], dlt_in.at[x], dlt_ssem.at[o], dlt_rsem.at[o], (row0 + c, t)
        )
        copy.start()
        dlt_copies.append(copy)
    sends += dlt_copies

    au_load.wait()
    own_sum = (bc[x, 0].astype(F32) + bc[x, 1].astype(F32)) + (
        bc[x, 2].astype(F32) + bc[x, 3].astype(F32)
    )
    ranks = jnp.where(lane < RANK, pltpu.roll(own_sum, RANK, 1), own_sum)
    spread = jnp.concatenate(
        [
            jnp.where((lane // RANK + 2 * n == slot_col) & resident, ranks, 0.0)
            for n in range(SLOTS // 2)
        ],
        axis=1,
    ).astype(BF16)
    acc = dot(spread, aup[...])

    folded = move.total()
    moved_sum = jnp.concatenate([folded[:8], folded[8:]], axis=1)
    high = moved_sum.astype(BF16)
    low = (moved_sum - high.astype(F32)).astype(BF16)
    both = jnp.concatenate([high, low], axis=0)
    l16 = iota((REQ, 16), 1) % 8
    into = jnp.full((REQ, 16), -1, jnp.int32)
    for j in range(SPAN * CAP):
        into = jnp.where(l16 == j, recv_s[0, j], into)
    replaced = dot((into == iota((REQ, 16), 0)).astype(BF16), both)
    acc = acc + jnp.where(taken, replaced, stay.total())
    for copy in dlt_copies:
        copy.wait_recv()
    out_ref[...] = (
        acc + jnp.concatenate([dlt_in[h].astype(F32) for h in range(ROW)], axis=1)
    ).astype(BF16)

    msg_copy.wait_send()
    for copy in stay.sib_copies + stay.copies + move.sib_copies + move.copies + sends:
        copy.wait_send()
    for copy, device in own_results:

        @pl.when(device != r)
        def _():
            copy.wait_send()


def body(
    queries,
    k_cache,
    v_cache,
    new_keys,
    new_values,
    kv_len,
    send_rows,
    recv_rows,
    out_weight,
    adapter_down,
    adapter_up,
    sectioned_down,
    sectioned_up,
    install,
    adapter_slot,
):
    vmem = pl.BlockSpec(memory_space=pltpu.VMEM)
    hbm = pl.BlockSpec(memory_space=pltpu.HBM)
    smem = functools.partial(pltpu.SMEM, dtype=jnp.int32)
    dma = pltpu.SemaphoreType.DMA
    lengths = kv_len.reshape(1, REQ)
    return pl.pallas_call(
        kernel,
        out_shape=jax.ShapeDtypeStruct((REQ, OUT), BF16),
        in_specs=[hbm] * 15,
        out_specs=vmem,
        scratch_shapes=[
            pltpu.VMEM((REQ, QW), BF16),
            pltpu.VMEM((REQ, HD), BF16),
            pltpu.VMEM((REQ, HD), BF16),
            pltpu.VMEM((1, REQ), jnp.int32),
            pltpu.VMEM((1, REQ), jnp.int32),
            smem((1, REQ)),
            smem((1, SPAN * CAP)),
            smem((1, SPAN * CAP)),
            smem((1, SLOTS)),
            pltpu.VMEM((REQ, LMAX, HD), BF16),
            pltpu.VMEM((REQ, LMAX, HD), BF16),
            pltpu.VMEM((TP * OUT, QW), BF16),
            pltpu.VMEM((SLOTS * RANK, QW), BF16),
            pltpu.VMEM((SLOTS * RANK, OUT), BF16),
            pltpu.VMEM((REP * RANK_PART, QW), BF16),
            pltpu.VMEM((REP * RANK, OUT_PART), BF16),
            pltpu.VMEM((SPAN, 16, HD), BF16),
            pltpu.VMEM((SPAN, 16, HD), BF16),
            pltpu.VMEM((ROW, 8, 128), jnp.int32),
            pltpu.VMEM((SPAN, 8, HD), F32),
            pltpu.VMEM((ROW, 32, HD), F32),
            pltpu.VMEM((ROW * REQ, QW), BF16),
            pltpu.VMEM((256, HD), F32),
            pltpu.VMEM((5 * 512, 128), BF16),
            pltpu.VMEM((512, 512), BF16),
            pltpu.VMEM((1, REQ, 128), BF16),
            pltpu.VMEM((REQ, 128), BF16),
            pltpu.VMEM((4, 4, REQ, 128), BF16),
            pltpu.VMEM((ROW * REQ, REP * RANK), BF16),
            pltpu.VMEM((ROW, REQ, OUT_PART), BF16),
            pltpu.VMEM((ROW, REQ, OUT_PART), BF16),
            pltpu.VMEM((4, REQ, OUT), BF16),
            pltpu.VMEM((4, REQ, OUT), BF16),
            pltpu.VMEM((4, REQ, OUT), F32),
            pltpu.VMEM((3, REQ, OUT), BF16),
            pltpu.VMEM((3, REQ, OUT), BF16),
            pltpu.VMEM((4, 16, OUT // 2), BF16),
            pltpu.VMEM((4, 16, OUT // 2), BF16),
            pltpu.VMEM((4, 16, OUT // 2), F32),
            pltpu.VMEM((3, 16, OUT // 2), BF16),
            pltpu.VMEM((3, 16, OUT // 2), BF16),
            dma((9,)),
            dma((5,)),
            dma((2,)),
            dma((4, 4)),
            dma((4, 4)),
            dma((4, 4)),
            dma((4, 4)),
            dma((4,)),
            dma((4,)),
            dma((4,)),
            dma((4,)),
            dma((4, 4)),
            dma((4, 4)),
            dma((4,)),
            dma((4,)),
            dma((2,)),
            dma((4, 4)),
            dma((4, 4)),
            dma((4,)),
            dma((4,)),
            dma((4,)),
            dma((4,)),
            dma((4,)),
            dma((4,)),
            dma((4,)),
            dma((4,)),
            dma((4,)),
            dma((4,)),
        ],
        compiler_params=pltpu.CompilerParams(
            collective_id=0, has_side_effects=True, vmem_limit_bytes=60 << 20
        ),
    )(
        queries,
        k_cache,
        v_cache,
        new_keys,
        new_values,
        lengths,
        adapter_slot.reshape(1, REQ),
        send_rows,
        recv_rows,
        install,
        out_weight,
        adapter_down.reshape(SLOTS * RANK, QW),
        adapter_up.reshape(SLOTS * RANK, OUT),
        sectioned_down.reshape(RANK, QW),
        sectioned_up.reshape(RANK, OUT),
    )


def solution(mesh):
    placed = (
        P("rep", "tp"),
        P("rep", None, "tp"),
        P("rep", None, "tp"),
        P("rep", "tp"),
        P("rep", "tp"),
        P("rep"),
        P("rep", None),
        P("rep", None),
        P(None, "tp"),
        P("rep", None, "tp"),
        P("rep", None, "tp"),
        P("rep", None, "tp"),
        P("rep", None, "tp"),
        P("rep", None),
        P("rep"),
    )
    return jax.shard_map(
        body, mesh=mesh, in_specs=placed, out_specs=P("rep", "tp"), check_vma=False
    )
```

```python
import functools

import jax
import jax.numpy as jnp
from jax import lax
from jax.experimental import pallas as pl
from jax.experimental.pallas import tpu as pltpu
from jax.sharding import PartitionSpec as P

MESH = pl.DeviceIdType.MESH
F32 = jnp.float32
BF16 = jnp.bfloat16

HD = 128
HEADS = 4
REQ = 32
LMAX = 128
RANK = 64
SLOTS = 8
SPAN = 4
CAP = 2
REP = 32
TP = 8
ROW = 4
QW = HEADS * HD
OUT = 1024
RANK_PART = RANK // ROW
OUT_PART = OUT // ROW
SCALE = HD**-0.5
DISTANCES = (1, 8, 12, 16)
FAR_FIRST = (2, 0, 3, 1)


def iota(shape, dim):
    return lax.broadcasted_iota(jnp.int32, shape, dim)


def dot(a, b):
    return lax.dot_general(a, b, (((1,), (0,)), ((), ())), preferred_element_type=F32)


def dot_nt(a, b):
    return lax.dot_general(a, b, (((1,), (1,)), ((), ())), preferred_element_type=F32)


def remote(src, dst, ssem, rsem, device):
    return pltpu.make_async_remote_copy(
        src_ref=src,
        dst_ref=dst,
        send_sem=ssem,
        recv_sem=rsem,
        device_id=device,
        device_id_type=MESH,
    )


def hops(offset):
    dy, dx = offset // 8, offset % 4
    return min(dy, 4 - dy) + min(dx, 4 - dx) + 4 * ((offset // 4) % 2)


def softmax_parts(scores, own, live):
    scores = jnp.where(live, scores * SCALE, -jnp.inf)
    own = own * SCALE
    top = jnp.maximum(jnp.max(scores, axis=1, keepdims=True), own)
    weights = jnp.exp(scores - top)
    own_weight = jnp.exp(own - top)
    total = jnp.sum(weights, axis=1, keepdims=True) + own_weight
    return weights.astype(BF16), own_weight.astype(BF16).astype(F32), total


def to_column(row, rows):
    spread = jnp.where(iota((rows, 128), 0) == iota((rows, 128), 1), row, 0)
    return jnp.sum(spread.astype(F32), axis=1, keepdims=True).astype(jnp.int32)


def kernel(
    q_hbm,
    k_hbm,
    v_hbm,
    nk_hbm,
    nv_hbm,
    len_hbm,
    slot_hbm,
    send_hbm,
    recv_hbm,
    install_hbm,
    w_hbm,
    adown_hbm,
    aup_hbm,
    sdown_hbm,
    sup_hbm,
    out_ref,
    q_ref,
    nk_ref,
    nv_ref,
    len_row,
    slot_row,
    len_s,
    send_s,
    recv_s,
    install_s,
    kbuf,
    vbuf,
    wbuf,
    adown,
    aup,
    sdn,
    sup,
    qout,
    qin,
    meta,
    res,
    mig,
    merged,
    obuf,
    fold,
    perm,
    msg,
    msg_sib,
    bc,
    sexp,
    dlt_out,
    dlt_in,
    sib_out,
    sib_in,
    rs_own,
    rs_out,
    rs_in,
    sib2_out,
    sib2_in,
    rs2_own,
    rs2_out,
    rs2_in,
    small_sem,
    load_sem,
    s1_local,
    s1_ssem,
    s1_rsem,
    s2_ssem,
    s2_rsem,
    q_ssem,
    q_rsem,
    meta_ssem,
    meta_rsem,
    mig_ssem,
    mig_rsem,
    loc_ssem,
    loc_rsem,
    msg_sem,
    bc_ssem,
    bc_rsem,
    dlt_ssem,
    dlt_rsem,
    sib_ssem,
    sib_rsem,
    rs_ssem,
    rs_rsem,
    sib2_ssem,
    sib2_rsem,
    rs2_ssem,
    rs2_rsem,
):
    r = lax.axis_index("rep")
    t = lax.axis_index("tp")
    x = r % 4
    zh = (r // 4) % 2
    y = r // 8
    row0 = r - x
    z = t // 2
    core = t % 2
    sib = (r, t + 1 - 2 * core)

    other0 = y * 8 + (1 - zh) * 4
    greeted = [((r + o) % REP, t) for o in sorted(range(1, REP), key=hops, reverse=True)]
    greeted += [
        (row0 + (x + xo) % 4, ((z + zo) % 4) * 2 + core)
        for xo in (2, 1, 3, 0)
        for zo in (2, 1, 3)
    ]
    greeted.append(sib)
    barrier = pltpu.get_barrier_semaphore()
    for peer in greeted:
        pl.semaphore_signal(barrier, inc=1, device_id=peer, device_id_type=MESH)

    small = [
        pltpu.make_async_copy(src, dst, small_sem.at[n])
        for n, (src, dst) in enumerate(
            (
                (q_hbm, q_ref),
                (nk_hbm, nk_ref),
                (nv_hbm, nv_ref),
                (recv_hbm, recv_s),
                (install_hbm, install_s),
                (slot_hbm, slot_row),
                (len_hbm, len_row),
                (len_hbm, len_s),
                (send_hbm, send_s),
            )
        )
    ]
    for copy in small:
        copy.start()
    k_load = pltpu.make_async_copy(k_hbm, kbuf, load_sem.at[0])
    v_load = pltpu.make_async_copy(v_hbm, vbuf, load_sem.at[1])
    ad_load = pltpu.make_async_copy(adown_hbm, adown, load_sem.at[2])
    w_load = pltpu.make_async_copy(w_hbm, wbuf, load_sem.at[3])
    au_load = pltpu.make_async_copy(aup_hbm, aup, load_sem.at[4])
    for copy in (k_load, v_load, ad_load, w_load, au_load):
        copy.start()
    for copy in small:
        copy.wait()

    queries = q_ref[...]
    q_heads = jnp.concatenate(
        [queries[:, h * HD : (h + 1) * HD] for h in range(HEADS)], axis=0
    )
    new_keys = nk_ref[...]
    new_values = nv_ref[...]
    stacked = jnp.concatenate([q_heads, new_keys, new_values], axis=0)
    line = iota((64, 192), 0)
    place = line % 16
    col = iota((64, 192), 1)
    kind = jnp.where(
        place < 8,
        place % 4,
        jnp.where(place < 10, 4, jnp.where(place < 12, 5, 9)),
    )
    within = jnp.where(place < 8, place // 4, place % 2)
    entry = (line // 16) * CAP + within
    wanted = jnp.full((64, 192), -1, jnp.int32)
    for j in range(SPAN * CAP):
        wanted = jnp.where(entry == j, recv_s[0, j], wanted)
    pick = (kind == col // REQ) & (wanted == col % REQ)
    gathered = dot(pick.astype(BF16), stacked).astype(BF16)
    for g in range(SPAN):
        qout[g] = gathered[g * 16 : (g + 1) * 16]

    lane1 = iota((1, 128), 1)
    recv4 = jnp.full((1, 128), -1, jnp.int32)
    for j in range(SPAN * CAP):
        recv4 = jnp.where(lane1 // 4 == j, recv_s[0, j], recv4)
    slots = slot_row[...]
    target = jnp.full((1, REQ), -1, jnp.int32)
    for k in range(SLOTS):
        target = jnp.where(slots == k, install_s[0, k], target)
    target = jnp.concatenate([target, jnp.full((1, 128 - REQ), -1, jnp.int32)], axis=1)
    sub8 = iota((8, 128), 0)
    meta[x] = jnp.where(sub8 == 0, recv4, jnp.where(sub8 == 1, target, -1))

    pl.semaphore_wait(barrier, len(greeted))

    sends = []

    q_copies = []
    for g in FAR_FIRST:
        copy = remote(
            qout.at[g],
            qin.at[g],
            q_ssem.at[g],
            q_rsem.at[g],
            ((r + REP - DISTANCES[g]) % REP, t),
        )
        copy.start()
        q_copies.append(copy)
    sends += q_copies

    my_dn = pl.ds(pl.multiple_of(r * RANK_PART, RANK_PART), RANK_PART)
    my_up = pl.ds(pl.multiple_of(r * RANK, RANK), RANK)

    def dn_part(c):
        return sdown_hbm.at[pl.ds(pl.multiple_of(c * RANK_PART, RANK_PART), RANK_PART)]

    def up_part(c):
        return sup_hbm.at[:, pl.ds(pl.multiple_of(c * OUT_PART, OUT_PART), OUT_PART)]

    own_dn = pltpu.make_async_copy(dn_part(x), sdn.at[my_dn], s1_local.at[0])
    own_up = pltpu.make_async_copy(up_part(x), sup.at[my_up], s1_local.at[1])
    own_dn.start()
    own_up.start()
    near_dn, near_up, far_dn, far_up = [], [], [], []
    for o in range(1, 4):
        c = (x + o) % 4
        near_dn.append(
            remote(dn_part(c), sdn.at[my_dn], s1_ssem.at[0, o], s1_rsem.at[0, o], (row0 + c, t))
        )
        near_up.append(
            remote(up_part(c), sup.at[my_up], s1_ssem.at[1, o], s1_rsem.at[1, o], (row0 + c, t))
        )
    for o in range(4):
        c = (x + o) % 4
        far_dn.append(
            remote(dn_part(c), sdn.at[my_dn], s1_ssem.at[2, o], s1_rsem.at[2, o], (other0 + c, t))
        )
        far_up.append(
            remote(up_part(c), sup.at[my_up], s1_ssem.at[3, o], s1_rsem.at[3, o], (other0 + c, t))
        )
    for copy in far_dn + near_dn + near_up:
        copy.start()
    sends += near_dn + near_up + far_dn + far_up

    meta_copies = []
    for o in range(1, 4):
        copy = remote(
            meta.at[x], meta.at[x], meta_ssem.at[o], meta_rsem.at[o], (row0 + (x + o) % 4, t)
        )
        copy.start()
        meta_copies.append(copy)
    sends += meta_copies

    def stage2(half, tag):
        first = y * 8 + half * 4
        dn_rows = pl.ds(pl.multiple_of(first * RANK_PART, 4 * RANK_PART), 4 * RANK_PART)
        up_rows = pl.ds(pl.multiple_of(first * RANK, 4 * RANK), 4 * RANK)
        dn, up = [], []
        for o in range(1, 4):
            peer = ((r + 8 * o) % REP, t)
            dn.append(
                remote(
                    sdn.at[dn_rows], sdn.at[dn_rows], s2_ssem.at[tag, o], s2_rsem.at[tag, o], peer
                )
            )
            up.append(
                remote(
                    sup.at[up_rows],
                    sup.at[up_rows],
                    s2_ssem.at[2 + tag, o],
                    s2_rsem.at[2 + tag, o],
                    peer,
                )
            )
        return dn, up

    s2_near_dn, s2_near_up = stage2(zh, 0)
    s2_far_dn, s2_far_up = stage2(1 - zh, 1)
    sends += s2_near_dn + s2_near_up + s2_far_dn + s2_far_up

    order = (2, 1, 3, 0)

    class Wave:
        def __init__(self, rows, own, sib_out, sib_in, out, arriving, sems):
            self.rows, self.own, self.out, self.arriving = rows, own, out, arriving
            self.sib_out, self.sib_in, self.sems = sib_out, sib_in, sems
            self.sib_copies, self.copies = [], []

        def project(self, zq, cq):
            first = pl.multiple_of((zq * 2 + cq) * OUT, OUT)
            return dot_nt(self.rows, wbuf[pl.ds(first, OUT), :])

        def opposite(self, n):
            self.sib_out[n] = self.fit(self.project((z + order[n]) % 4, 1 - core)).astype(BF16)
            copy = remote(
                self.sib_out.at[n], self.sib_in.at[n], self.sems[0].at[n], self.sems[1].at[n], sib
            )
            copy.start()
            self.sib_copies.append(copy)

        def same(self, n):
            self.own[n] = self.fit(self.project((z + order[n]) % 4, core))

        def pass_on(self, n):
            zq = (z + order[n]) % 4
            self.sib_copies[n].wait_recv()
            both = self.own[n] + self.sib_in[n].astype(F32)
            if order[n] == 0:
                self.own[n] = both
                return
            self.out[n] = both.astype(BF16)
            copy = remote(
                self.out.at[n],
                self.arriving.at[n],
                self.sems[2].at[n],
                self.sems[3].at[n],
                (r, zq * 2 + core),
            )
            copy.start()
            self.copies.append(copy)

        def total(self):
            acc = self.own[3]
            for n, copy in enumerate(self.copies):
                copy.wait_recv()
                acc = acc + self.arriving[n].astype(F32)
            return acc

        def fit(self, block):
            if block.shape[0] == REQ:
                return block
            return jnp.concatenate([block[:8, : OUT // 2], block[:8, OUT // 2 :]], axis=0)

    own_dn.wait()
    for copy in near_dn:
        copy.wait_recv()
    for copy in s2_near_dn:
        copy.start()

    k_load.wait()
    for copy in far_up:
        copy.start()
    for copy in q_copies:
        copy.wait_recv()
    head8 = iota((8, HD), 0) // HEADS == 0
    line32 = iota((32, 128), 0) // HEADS
    moved_len = jnp.zeros((32, 128), jnp.int32)
    moved_scores, moved_own, moved_values, places = [], [], [], []
    for g in range(SPAN):
        arrived = qin[g]
        arrived_f = arrived.astype(F32)
        q8 = arrived[0:8]
        parts = []
        for i in range(CAP):
            j = g * CAP + i
            at = jnp.maximum(send_s[0, j], 0)
            places.append(at)
            parts.append(dot_nt(q8, kbuf[at]))
            moved_len = jnp.where(line32 == j, len_s[0, at], moved_len)
        moved_scores.append(jnp.where(head8, parts[0], parts[1]))
        key = jnp.where(head8, arrived_f[8:9], arrived_f[9:10])
        moved_own.append(jnp.sum(arrived_f[0:8] * key, axis=1, keepdims=True))
        moved_values.append(jnp.where(head8, arrived_f[10:11], arrived_f[11:12]))
    m_weights, m_own, m_total = softmax_parts(
        jnp.concatenate(moved_scores, axis=0),
        jnp.concatenate(moved_own, axis=0),
        iota((32, 128), 1) < moved_len,
    )
    v_load.wait()
    m_summed = []
    m_wf = m_weights.astype(F32)
    for g in range(SPAN):
        w8 = m_wf[g * 8 : (g + 1) * 8].astype(BF16)
        a = dot(w8, vbuf[places[g * CAP]])
        b = dot(w8, vbuf[places[g * CAP + 1]])
        m_summed.append(jnp.where(head8, a, b))
    m_out = (
        jnp.concatenate(m_summed, axis=0) + m_own * jnp.concatenate(moved_values, axis=0)
    ) / m_total
    m_out = m_out.astype(BF16).astype(F32)
    for g in range(SPAN):
        res[g] = m_out[g * 8 : (g + 1) * 8]

    own_results = []
    for g in FAR_FIRST:
        home = (r + DISTANCES[g]) % REP
        home_x = home % 4
        dst = mig.at[home_x, pl.ds(8 * g, 8)]
        for o in (2, 1, 3, 0):
            device = home - home_x + (home_x + o) % 4
            copy = remote(
                res.at[g], dst, mig_ssem.at[g, o], mig_rsem.at[home_x, g], (device, t)
            )
            if g == 0 and o:
                stays = pltpu.make_async_copy(res.at[g], dst, mig_rsem.at[home_x, g])

                @pl.when(device == r)
                def _():
                    stays.start()

                @pl.when(device != r)
                def _():
                    copy.start()

                own_results.append((copy, device))
            else:
                copy.start()
                sends.append(copy)

    er = iota((256, 128), 0)
    ec = iota((256, 128), 1)
    spread_q = ((er % 8 == ec // REQ) & (er // 8 == ec % REQ)).astype(BF16)
    q_local = dot(spread_q, q_heads)
    spread_r = iota((256, REQ), 0) // 8 == iota((256, REQ), 1)
    new_kv = dot(spread_r.astype(BF16), jnp.concatenate([new_keys, new_values], axis=1))
    lengths = jnp.sum(
        jnp.where(spread_r, len_row[...], 0).astype(F32), axis=1, keepdims=True
    ).astype(jnp.int32)
    scores = lax.dot_general(
        q_local.reshape(REQ, 8, HD).astype(BF16),
        kbuf[...],
        (((2,), (2,)), ((0,), (0,))),
        preferred_element_type=F32,
    ).reshape(256, LMAX)
    own = jnp.sum(q_local * new_kv[:, :HD], axis=1, keepdims=True)
    weights, own_b, total = softmax_parts(scores, own, ec < lengths)
    summed = lax.dot_general(
        weights.reshape(REQ, 8, LMAX),
        vbuf[...],
        (((2,), (1,)), ((0,), (0,))),
        preferred_element_type=F32,
    ).reshape(256, HD)
    obuf[...] = (summed + own_b * new_kv[:, HD:]) / total
    here = jnp.concatenate(
        [obuf[pl.ds(h, REQ, stride=8), :] for h in range(HEADS)], axis=1
    ).astype(BF16)

    fc = iota((5 * 512, 128), 0)
    fl = iota((5 * 512, 128), 1)
    block = fc // 512
    goal = jnp.where(block < 4, block * RANK_PART + fc % RANK_PART, 64 + fc % RANK)
    fold[...] = (fl == goal).astype(BF16)
    pc = iota((512, 512), 0)
    pj = iota((512, 512), 1)
    inner = pc % 128
    hit = (
        (inner < 64)
        & (inner // RANK_PART == pj // 128)
        & (pj % 64 == (pc // 128) * RANK_PART + pc % RANK_PART)
    )
    perm[...] = hit.astype(BF16)

    my_rows = pl.ds(pl.multiple_of(x * REQ, REQ), REQ)
    merged[my_rows, :] = here
    row_copies = []
    for o in (2, 1, 3):
        copy = remote(
            merged.at[my_rows],
            merged.at[my_rows],
            loc_ssem.at[o],
            loc_rsem.at[o],
            (row0 + (x + o) % 4, t),
        )
        copy.start()
        row_copies.append(copy)
    sends += row_copies
    stay = Wave(
        here, rs_own, sib_out, sib_in, rs_out, rs_in, (sib_ssem, sib_rsem, rs_ssem, rs_rsem)
    )
    w_load.wait()
    stay.opposite(0)
    stay.same(0)

    for copy in far_dn:
        copy.wait_recv()
    for copy in s2_far_dn:
        copy.start()
    own_up.wait()
    for copy in near_up:
        copy.wait_recv()
    for copy in s2_near_up:
        copy.start()

    stay.opposite(1)
    stay.pass_on(0)
    stay.same(1)
    stay.opposite(2)
    stay.pass_on(1)
    stay.same(2)
    stay.pass_on(2)

    def arrived_at(h):
        for g in range(SPAN):
            remote(
                res.at[0], mig.at[h, pl.ds(8 * g, 8)], mig_ssem.at[g, 0], mig_rsem.at[h, g], sib
            ).wait_recv()

    mh = iota((128, 32), 0)
    ml = iota((128, 32), 1)

    def put_rows(recv_row, results, rows):
        put = ((mh % REQ == recv_row) & (mh // REQ == ml % 4)).astype(BF16)
        placed = dot(put, results.astype(BF16)).astype(BF16)
        placed = jnp.concatenate([placed[k * REQ : (k + 1) * REQ] for k in range(HEADS)], axis=1)
        hit = jnp.where(iota((REQ, 32), 0) == recv_row, 1.0, 0.0)
        taken = jnp.max(hit, axis=1, keepdims=True) > 0.5
        return jnp.where(taken, placed, rows), taken

    arrived_at(x)
    mine, taken = put_rows(recv4[:, 0:32], mig[x], here)
    moved = jnp.concatenate([mig[x, pl.ds(h, 8, stride=HEADS), :] for h in range(HEADS)], axis=1)
    moved = jnp.concatenate([moved, jnp.zeros_like(moved)], axis=0).astype(BF16)
    move = Wave(
        moved,
        rs2_own,
        sib2_out,
        sib2_in,
        rs2_out,
        rs2_in,
        (sib2_ssem, sib2_rsem, rs2_ssem, rs2_rsem),
    )

    ad_load.wait()
    slot_col = to_column(
        jnp.concatenate([slots, jnp.full((1, 128 - REQ), -1, jnp.int32)], axis=1), REQ
    )
    resident = to_column(target, REQ) < 0
    c512 = iota((REQ, 512), 1)
    part = dot_nt(mine, adown[...])
    pieces = [jnp.where((c512 // RANK == slot_col) & resident, part, 0.0)]
    for copy in meta_copies + row_copies:
        copy.wait_recv()
    for o in range(1, 4):
        arrived_at((x + o) % 4)
    tiles = [meta[h] for h in range(ROW)]
    tcols = [to_column(tile[1:2], REQ) for tile in tiles]
    together = jnp.concatenate(
        [
            put_rows(tiles[h][0:1, 0:32], mig[h], merged[h * REQ : (h + 1) * REQ, :])[0]
            for h in range(ROW)
        ],
        axis=0,
    )
    for copy in s2_near_dn + s2_far_dn:
        copy.wait_recv()
    part = dot_nt(together, sdn[...])
    sections = [
        jnp.where(c512 // RANK_PART == tcols[h], part[h * REQ : (h + 1) * REQ], 0.0)
        for h in range(ROW)
    ]
    masked = jnp.concatenate(sections + pieces, axis=1).astype(BF16)
    msg[0] = dot(masked, fold[...]).astype(BF16)
    msg_copy = remote(msg.at[0], msg_sib, msg_sem.at[0], msg_sem.at[1], sib)
    msg_copy.start()
    for copy in far_up:
        copy.wait_recv()
    for copy in s2_far_up:
        copy.start()
    move.opposite(0)
    move.same(0)
    msg_copy.wait_recv()
    bc[x, z] = (msg[0].astype(F32) + msg_sib[...].astype(F32)).astype(BF16)
    bc_copies = []
    for xo in range(4):
        for zo in range(4):
            if xo == 0 and zo == 0:
                continue
            copy = remote(
                bc.at[x, z],
                bc.at[x, z],
                bc_ssem.at[xo, zo],
                bc_rsem.at[xo, zo],
                (row0 + (x + xo) % 4, ((z + zo) % 4) * 2 + core),
            )
            copy.start()
            bc_copies.append(copy)
    sends += bc_copies
    move.pass_on(0)
    stay.opposite(3)
    stay.same(3)
    stay.pass_on(3)
    for n in range(1, 4):
        move.opposite(n)
        move.same(n)
        move.pass_on(n)

    for copy in bc_copies:
        copy.wait_recv()
    sums = []
    for h in range(ROW):
        sums.append(
            (bc[h, 0].astype(F32) + bc[h, 1].astype(F32))
            + (bc[h, 2].astype(F32) + bc[h, 3].astype(F32))
        )
    shrunk = dot(jnp.concatenate(sums, axis=1).astype(BF16), perm[...])
    lane = iota((REQ, 128), 1)
    for h in range(ROW):
        ranks = shrunk[:, h * 128 : (h + 1) * 128]
        for n in range(16):
            sexp[h * REQ : (h + 1) * REQ, n * 128 : (n + 1) * 128] = jnp.where(
                lane // RANK + 2 * n == tcols[h], ranks, 0.0
            ).astype(BF16)
    for copy in s2_near_up + s2_far_up:
        copy.wait_recv()
    delta = dot(sexp[...], sup[...])
    dlt_copies = []
    for h in range(ROW):
        dlt_out[h] = delta[h * REQ : (h + 1) * REQ].astype(BF16)
    dlt_in[x] = dlt_out[x]
    for o in range(1, 4):
        c = (x + o) % 4
        copy = remote(
            dlt_out.at[c], dlt_in.at[x], dlt_ssem.at[o], dlt_rsem.at[o], (row0 + c, t)
        )
        copy.start()
        dlt_copies.append(copy)
    sends += dlt_copies

    au_load.wait()
    own_sum = (bc[x, 0].astype(F32) + bc[x, 1].astype(F32)) + (
        bc[x, 2].astype(F32) + bc[x, 3].astype(F32)
    )
    ranks = jnp.where(lane < RANK, pltpu.roll(own_sum, RANK, 1), own_sum)
    spread = jnp.concatenate(
        [
            jnp.where((lane // RANK + 2 * n == slot_col) & resident, ranks, 0.0)
            for n in range(SLOTS // 2)
        ],
        axis=1,
    ).astype(BF16)
    acc = dot(spread, aup[...])

    folded = move.total()
    moved_sum = jnp.concatenate([folded[:8], folded[8:]], axis=1)
    high = moved_sum.astype(BF16)
    low = (moved_sum - high.astype(F32)).astype(BF16)
    both = jnp.concatenate([high, low], axis=0)
    l16 = iota((REQ, 16), 1) % 8
    into = jnp.full((REQ, 16), -1, jnp.int32)
    for j in range(SPAN * CAP):
        into = jnp.where(l16 == j, recv_s[0, j], into)
    replaced = dot((into == iota((REQ, 16), 0)).astype(BF16), both)
    acc = acc + jnp.where(taken, replaced, stay.total())
    for copy in dlt_copies:
        copy.wait_recv()
    out_ref[...] = (
        acc + jnp.concatenate([dlt_in[h].astype(F32) for h in range(ROW)], axis=1)
    ).astype(BF16)

    msg_copy.wait_send()
    for copy in stay.sib_copies + stay.copies + move.sib_copies + move.copies + sends:
        copy.wait_send()
    for copy, device in own_results:

        @pl.when(device != r)
        def _():
            copy.wait_send()


def body(
    queries,
    k_cache,
    v_cache,
    new_keys,
    new_values,
    kv_len,
    send_rows,
    recv_rows,
    out_weight,
    adapter_down,
    adapter_up,
    sectioned_down,
    sectioned_up,
    install,
    adapter_slot,
):
    vmem = pl.BlockSpec(memory_space=pltpu.VMEM)
    hbm = pl.BlockSpec(memory_space=pltpu.HBM)
    smem = functools.partial(pltpu.SMEM, dtype=jnp.int32)
    dma = pltpu.SemaphoreType.DMA
    lengths = kv_len.reshape(1, REQ)
    return pl.pallas_call(
        kernel,
        out_shape=jax.ShapeDtypeStruct((REQ, OUT), BF16),
        in_specs=[hbm] * 15,
        out_specs=vmem,
        scratch_shapes=[
            pltpu.VMEM((REQ, QW), BF16),
            pltpu.VMEM((REQ, HD), BF16),
            pltpu.VMEM((REQ, HD), BF16),
            pltpu.VMEM((1, REQ), jnp.int32),
            pltpu.VMEM((1, REQ), jnp.int32),
            smem((1, REQ)),
            smem((1, SPAN * CAP)),
            smem((1, SPAN * CAP)),
            smem((1, SLOTS)),
            pltpu.VMEM((REQ, LMAX, HD), BF16),
            pltpu.VMEM((REQ, LMAX, HD), BF16),
            pltpu.VMEM((TP * OUT, QW), BF16),
            pltpu.VMEM((SLOTS * RANK, QW), BF16),
            pltpu.VMEM((SLOTS * RANK, OUT), BF16),
            pltpu.VMEM((REP * RANK_PART, QW), BF16),
            pltpu.VMEM((REP * RANK, OUT_PART), BF16),
            pltpu.VMEM((SPAN, 16, HD), BF16),
            pltpu.VMEM((SPAN, 16, HD), BF16),
            pltpu.VMEM((ROW, 8, 128), jnp.int32),
            pltpu.VMEM((SPAN, 8, HD), F32),
            pltpu.VMEM((ROW, 32, HD), F32),
            pltpu.VMEM((ROW * REQ, QW), BF16),
            pltpu.VMEM((256, HD), F32),
            pltpu.VMEM((5 * 512, 128), BF16),
            pltpu.VMEM((512, 512), BF16),
            pltpu.VMEM((1, REQ, 128), BF16),
            pltpu.VMEM((REQ, 128), BF16),
            pltpu.VMEM((4, 4, REQ, 128), BF16),
            pltpu.VMEM((ROW * REQ, REP * RANK), BF16),
            pltpu.VMEM((ROW, REQ, OUT_PART), BF16),
            pltpu.VMEM((ROW, REQ, OUT_PART), BF16),
            pltpu.VMEM((4, REQ, OUT), BF16),
            pltpu.VMEM((4, REQ, OUT), BF16),
            pltpu.VMEM((4, REQ, OUT), F32),
            pltpu.VMEM((3, REQ, OUT), BF16),
            pltpu.VMEM((3, REQ, OUT), BF16),
            pltpu.VMEM((4, 16, OUT // 2), BF16),
            pltpu.VMEM((4, 16, OUT // 2), BF16),
            pltpu.VMEM((4, 16, OUT // 2), F32),
            pltpu.VMEM((3, 16, OUT // 2), BF16),
            pltpu.VMEM((3, 16, OUT // 2), BF16),
            dma((9,)),
            dma((5,)),
            dma((2,)),
            dma((4, 4)),
            dma((4, 4)),
            dma((4, 4)),
            dma((4, 4)),
            dma((4,)),
            dma((4,)),
            dma((4,)),
            dma((4,)),
            dma((4, 4)),
            dma((4, 4)),
            dma((4,)),
            dma((4,)),
            dma((2,)),
            dma((4, 4)),
            dma((4, 4)),
            dma((4,)),
            dma((4,)),
            dma((4,)),
            dma((4,)),
            dma((4,)),
            dma((4,)),
            dma((4,)),
            dma((4,)),
            dma((4,)),
            dma((4,)),
        ],
        compiler_params=pltpu.CompilerParams(
            collective_id=0, has_side_effects=True, vmem_limit_bytes=60 << 20
        ),
    )(
        queries,
        k_cache,
        v_cache,
        new_keys,
        new_values,
        lengths,
        adapter_slot.reshape(1, REQ),
        send_rows,
        recv_rows,
        install,
        out_weight,
        adapter_down.reshape(SLOTS * RANK, QW),
        adapter_up.reshape(SLOTS * RANK, OUT),
        sectioned_down.reshape(RANK, QW),
        sectioned_up.reshape(RANK, OUT),
    )


def solution(mesh):
    placed = (
        P("rep", "tp"),
        P("rep", None, "tp"),
        P("rep", None, "tp"),
        P("rep", "tp"),
        P("rep", "tp"),
        P("rep"),
        P("rep", None),
        P("rep", None),
        P(None, "tp"),
        P("rep", None, "tp"),
        P("rep", None, "tp"),
        P("rep", None, "tp"),
        P("rep", None, "tp"),
        P("rep", None),
        P("rep"),
    )
    return jax.shard_map(
        body, mesh=mesh, in_specs=placed, out_specs=P("rep", "tp"), check_vma=False
    )
```
